128 devices in a mesh: lon: 32 (over z, x_lo, y), lat: 4 (over x_hi, core).
Axes of the slice: x: 4 (x_hi: 2, x_lo: 2; x = x_hi * 2 + x_lo), y: 4, z: 4, core: 2. Of those that a mesh axis runs over, the one named last changes fastest.
Arguments:
- state: float32 [2, 8, 1024, 4096], P(None, None, 'lat', 'lon'), may hold values from -6 to 6
- blocks: float32 [16384, 2, 8, 128], P(('lon', 'lat')), may hold values from -6 to 6
- dest_tile: int32 [16384, 1], P(('lon', 'lat')), may hold values from 0 to 127; in each aligned block of 128 rows (0 to 127, 128 to 255, ...) at most 2 rows name the same one
- dest_row: int32 [16384], P(('lon', 'lat')), may hold values from 0 to 255
- kappa: float32 [8, 1024, 4096], P(None, 'lat', 'lon'), may hold values from 0.02 to 0.2
- lon_speed: float32 [8, 1024, 4096], P(None, 'lat', 'lon'), may hold values from -0.5 to 0.5
- lat_speed: float32 [8, 1024, 4096], P(None, 'lat', 'lon'), may hold values from -0.5 to 0.5
- sea_mask: int32 [8, 1024, 4096], P(None, 'lat', 'lon'), may hold values 0 or 1
Outputs:
- updated: float32 [2, 8, 1024, 4096], P(None, None, 'lat', 'lon')
The draws below stay inside these ranges and needn't reach their ends.
Inputs may be any that keep to these rules, and one draw needn't show every extreme that they name: `dest_tile`: among the 128 blocks of one analysis owner (aligned blocks of rows) no tile is named more than 2 times, and one tile is named exactly 2 times in some of them.
All inputs are finite; a program needn't handle non-finite values. No bound on the sum of `sea_mask` on one device may be relied on, other than what follows from the above.
Results may differ from the reference program's by a relative error of at most 0.000086.
Values sent between devices are 32-bit elements; how exact they have to be, the bound alone decides.
A program may use at most 128 MiB of HBM per device.

```python
import math
import jax
import jax.numpy as jnp
import numpy as np

TR = 2
LEV = 8
CLAT = 256
CLON = 128
NBLK_DEV = 128
STEPS = 3
NLAT = 1024
NLON = 4096
BLOCKS = 16384
CAP = 2
N_LON = 32
N_LAT = 4


def touch_ends(drawn, key, least, largest):
    spot = [jax.random.randint(jax.random.fold_in(key, axis), (), 0, length) for axis, length in enumerate(drawn.shape)]
    widest = drawn.shape.index(max(drawn.shape))
    beside = spot[:widest] + [(spot[widest] + 1) % drawn.shape[widest]] + spot[widest + 1:]
    return drawn.at[tuple(spot)].set(least).at[tuple(beside)].set(largest)


def block_scale(rng, shape, split, low, top_value):
    factor_of = 1.0
    for dim, parts in split:
        draws = jax.random.uniform(jax.random.fold_in(jax.random.fold_in(rng, 6), dim), (parts,), jnp.float32, low / len(split), top_value / len(split))
        factor_of = factor_of * jnp.repeat(jnp.exp(draws), shape[dim] // parts).reshape((-1,) + (1,) * (len(shape) - 1 - dim))
    return factor_of


def routed_block(stream_key, own, number, rows, number_of, top, bound, slope):
    sequence = jax.random.permutation(stream_key, number_of)
    packed, ordinary = portions_of(number_of, rows * top, bound, slope, True), portions_of(number_of, rows * top, bound, slope, False)
    places = jnp.arange(number_of)

    def named(tallies, turn):
        used = int((tallies > 0).sum())
        fixed = max(1, used // 4)
        passed = fixed + (places - fixed + turn * (used - fixed)) % max(1, number_of - fixed)
        return jnp.zeros((number_of,), jnp.int32).at[sequence[jnp.where(places < fixed, places, passed)]].set(jnp.asarray(tallies, jnp.int32))

    tallies = jnp.where(number % 4 == 0, named(packed, number // 4), named(ordinary, number - number // 4 - 1))
    mixed = jax.random.permutation(jax.random.fold_in(own, 3), number_of)
    giver, taker = mixed[0:number_of // 2 * 2:2], mixed[1:number_of // 2 * 2:2]
    slack = jnp.minimum(tallies[giver] - 1, bound - tallies[taker]) // 2
    slack = jnp.where((giver == sequence[0]) | (taker == sequence[0]) | (tallies[taker] == 0), 0, jnp.maximum(slack, 0))
    passed = jax.random.randint(jax.random.fold_in(own, 4), (number_of // 2,), 0, 1 << 20) % (slack + 1)
    tallies = tallies.at[giver].add(-passed).at[taker].add(passed)
    members = jnp.searchsorted(jnp.cumsum(tallies), jnp.arange(rows * top), side="right").astype(jnp.int32)
    table = members.reshape(top, rows).T
    table = table[jax.random.permutation(jax.random.fold_in(own, 1), rows)]
    turn = jax.random.randint(jax.random.fold_in(own, 2), (rows, 1), 0, top)
    return jnp.take_along_axis(table, (jnp.arange(top)[None, :] + turn) % top, axis=1)


def portions_of(count, total, reach, lean, full):
    weights = [(1 << 20) // math.isqrt(rank ** lean) + 1 for rank in range(1, count + 1)]
    largest = reach if full else min(reach, max(-(-total // count), total * weights[0] // sum(weights)))
    least = 1 if total - largest >= count - 1 else 0
    given, spare = [largest] + [least] * (count - 1), total - largest - least * (count - 1)
    while spare > 0:
        free = [i for i in range(1, count) if given[i] < largest] or [i for i in range(1, count) if given[i] < reach]
        mass, budget = sum([weights[i] for i in free]), spare
        for i in free:
            extra = min(reach - given[i], max(1, budget * weights[i] // mass), spare)
            given[i] = given[i] + extra
            spare = spare - extra
    return np.array(given)


def scatter_about(rng, dims, width, most, shards=(), kind=jnp.bfloat16):
    values = jax.random.normal(rng, dims, jnp.float32) * width
    if len(shards) > 0:
        values = block_scale(rng, dims, shards, -0.22, 0.18) * values
    return jnp.clip(values, min=-most, max=most).astype(kind)


def setup_inputs(seed: int = 0) -> dict:
    arg_keys = jax.random.split(jax.random.key(seed), 9)
    state = scatter_about(arg_keys[0], (TR, LEV, NLAT, NLON), 1.0, 6.0, ((2, 4), (3, 32)), jnp.float32)
    blocks = scatter_about(arg_keys[1], (BLOCKS, TR, LEV, CLON), 1.0, 6.0, ((0, 128),), jnp.float32)
    dest_tile_keys = jax.random.split(jax.random.fold_in(arg_keys[2], 1), BLOCKS // NBLK_DEV)
    dest_tile_turns = jax.random.permutation(jax.random.fold_in(arg_keys[2], 3), BLOCKS // NBLK_DEV)
    dest_tile = jax.vmap(lambda own, number: routed_block(jax.random.fold_in(arg_keys[2], 2), own, number, NBLK_DEV, N_LON * N_LAT, 1, CAP, 2))(dest_tile_keys, dest_tile_turns).reshape((BLOCKS, 1))
    dest_row = touch_ends(jax.random.randint(arg_keys[3], (BLOCKS,), 0, CLAT), jax.random.fold_in(arg_keys[3], 1), 0, CLAT - 1).astype(jnp.int32)
    kappa = jnp.clip(jnp.exp(math.log(0.2) - 2.3025851 * jax.random.uniform(arg_keys[4], (LEV, NLAT, NLON), jnp.float32) ** block_scale(arg_keys[4], (LEV, NLAT, NLON), ((1, 4), (2, 32)), -0.2, 0.2)), 0.02, 0.2)
    lon_speed = jnp.clip(jax.random.uniform(arg_keys[5], (LEV, NLAT, NLON), jnp.float32, -0.5, 0.5) * block_scale(arg_keys[5], (LEV, NLAT, NLON), ((1, 4), (2, 32)), -0.4, 0.0), -0.5, 0.5)
    lat_speed = jnp.clip(jax.random.uniform(arg_keys[6], (LEV, NLAT, NLON), jnp.float32, -0.5, 0.5) * block_scale(arg_keys[6], (LEV, NLAT, NLON), ((1, 4), (2, 32)), -0.4, 0.0), -0.5, 0.5)
    sea_mask = touch_ends((jax.random.randint(arg_keys[7], (LEV, NLAT, NLON), 0, 5) < 4).astype(jnp.int32), jax.random.fold_in(arg_keys[7], 1), 0, 1)
    return dict(state=state, blocks=blocks, dest_tile=dest_tile, dest_row=dest_row, kappa=kappa, lon_speed=lon_speed, lat_speed=lat_speed, sea_mask=sea_mask)


def advance(extended, diffusivity, zonal_speed, merid_speed, forcing):
    center = extended[:, :, 2:-2, 2:-2]
    east_cell = extended[:, :, 2:-2, 3:-1]
    west_cell = extended[:, :, 2:-2, 1:-3]
    far_east = extended[:, :, 2:-2, 4:]
    far_west = extended[:, :, 2:-2, :-4]
    north_cell = extended[:, :, 3:-1, 2:-2]
    south_cell = extended[:, :, 1:-3, 2:-2]
    far_north = extended[:, :, 4:, 2:-2]
    far_south = extended[:, :, :-4, 2:-2]
    laplace = east_cell + west_cell + north_cell + south_cell - 4.0 * center
    zonal = (8.0 * (east_cell - west_cell) - (far_east - far_west)) / 12.0
    meridional = (8.0 * (north_cell - south_cell) - (far_north - far_south)) / 12.0
    return center + diffusivity * laplace - zonal_speed * zonal - merid_speed * meridional + forcing


def reference(state, blocks, dest_tile, dest_row, kappa, lon_speed, lat_speed, sea_mask):
    tiles = dest_tile[:, 0].astype(jnp.int32)
    lat_rows = (tiles % N_LAT) * CLAT + dest_row.astype(jnp.int32)
    lon_tiles = tiles // N_LAT
    cells = lat_rows * N_LON + lon_tiles
    flat_blocks = blocks.reshape(BLOCKS, TR * LEV * CLON)
    summed = jax.ops.segment_sum(flat_blocks, cells, num_segments=NLAT * N_LON)
    increment = summed.reshape(NLAT, N_LON, TR, LEV, CLON).transpose(2, 3, 0, 1, 4).reshape(TR, LEV, NLAT, NLON)
    wet = sea_mask.astype(jnp.float32)
    diffusivity = kappa * wet
    zonal_speed = lon_speed * wet
    merid_speed = lat_speed * wet
    forcing = (increment * wet) / STEPS
    tracer = state
    for repeat in range(STEPS):
        wrapped = jnp.concatenate([tracer[:, :, :, -2:], tracer, tracer[:, :, :, :2]], axis=3)
        extended = jnp.pad(wrapped, ((0, 0), (0, 0), (2, 2), (0, 0)))
        tracer = advance(extended, diffusivity, zonal_speed, merid_speed, forcing)
    return tracer
```

```python
import functools

import jax
import jax.numpy as jnp
from jax import lax
from jax.experimental import pallas as pl
from jax.experimental.pallas import tpu as pltpu
from jax.sharding import PartitionSpec as P

MESH = pl.DeviceIdType.MESH
STEPS = 3
HALO = 8
BLOCK = 32
STRIDE = 37


def roll(x, amount):
    amount = amount % 128
    return x if amount == 0 else pltpu.roll(x, amount, 1)


def kernel(
    state, blocks, tile_at, row_at, kappa, lon_speed, lat_speed, mask, out,
    tile_ref, row_ref, q0, q1, q2, part, force, diff, zonal, merid, wet, held, table, table_s, plan, meta_out, meta_in,
    send, recv, lon_out, lon_in, load_sem, table_sem, send_sem, recv_sem, halo_send, halo_recv, out_sem,
):
    tracers, levels = send.shape[0], kappa.shape[0]
    rows = kappa.shape[1]
    lon, lat = lax.axis_index("lon"), lax.axis_index("lat")
    me = lon * 4 + lat

    moves = (
        (tile_at, tile_ref), (row_at, row_ref), (blocks, held), (state, q0.at[:, pl.ds(HALO, rows)]),
        (kappa, diff), (lon_speed, zonal), (lat_speed, merid), (mask, wet),
    )
    loads = [pltpu.make_async_copy(src, dst, load_sem.at[k]) for k, (src, dst) in enumerate(moves)]
    for copy in loads:
        copy.start()

    def partner(i):
        target = (me + i * STRIDE) % 128
        return (target // 4, target % 4)

    barrier = pltpu.get_barrier_semaphore()

    def greet(i, carry):
        pl.semaphore_signal(barrier, inc=1, device_id=partner(i), device_id_type=MESH)
        return carry

    lax.fori_loop(1, 128, greet, 0)
    loads[0].wait()
    loads[1].wait()

    tile_of = lax.broadcasted_iota(jnp.int32, (128, 128), 0)
    number = lax.broadcasted_iota(jnp.int32, (128, 128), 1)
    lane = number
    named = tile_ref[...] == tile_of
    first = jnp.min(jnp.where(named, number, 128), axis=1, keepdims=True)
    last = jnp.max(jnp.where(named, number, -1), axis=1, keepdims=True)
    row_f = row_ref[...].astype(jnp.float32)
    first_row = jnp.sum(jnp.where(number == first, row_f, 0.0), axis=1, keepdims=True)
    last_row = jnp.sum(jnp.where(number == last, row_f, 0.0), axis=1, keepdims=True)
    first_row = jnp.where(last >= 0, first_row, -1.0)
    last_row = jnp.where(last > first, last_row, -1.0)
    plan[...] = jnp.where(lane == 0, first_row, last_row)
    slots = jnp.where(lane == 0, jnp.minimum(first, 127), jnp.maximum(last, 0))
    table[...] = jnp.transpose(slots)[:8]
    to_scalars = pltpu.make_async_copy(table, table_s, table_sem)
    to_scalars.start()
    loads[2].wait()
    to_scalars.wait()

    def pack(i, carry):
        target = (me + i * STRIDE) % 128
        meta_out[i] = plan[pl.ds(target, 1), :]
        for s in range(2):
            block = held[table_s[s, target]]
            for t in range(tracers):
                send[t, i, pl.ds(s * levels, levels)] = block[t * levels : (t + 1) * levels]
        return carry

    lax.fori_loop(0, 128, pack, 0)

    pl.semaphore_wait(barrier, 127)

    def post(i, carry):
        pltpu.make_async_remote_copy(
            src_ref=meta_out.at[i], dst_ref=meta_in.at[i], send_sem=send_sem.at[tracers], recv_sem=recv_sem.at[tracers],
            device_id=partner(i), device_id_type=MESH,
        ).start()
        return carry

    lax.fori_loop(1, 128, post, 0)
    for t in range(tracers):

        def post_blocks(i, carry):
            pltpu.make_async_remote_copy(
                src_ref=send.at[t, i], dst_ref=recv.at[t, i], send_sem=send_sem.at[t], recv_sem=recv_sem.at[t],
                device_id=partner(i), device_id_type=MESH,
            ).start()
            return carry

        lax.fori_loop(1, 128, post_blocks, 0)
    meta_in[0] = meta_out[0]
    for t in range(tracers):
        recv[t, 0] = send[t, 0]

    east, west = ((lon + 1) % 32, lat), ((lon + 31) % 32, lat)
    wide = lax.broadcasted_iota(jnp.int32, (8, 128), 1)

    def edges(values, packed, k):
        return jnp.where(wide // 4 == k, roll(values, 4 * k + 2), packed)

    def halo_copies(q, step):
        many = q.shape[0]
        copies = []
        for d, device in enumerate((east, west)):
            copies.append(pltpu.make_async_remote_copy(
                src_ref=lon_out.at[step], dst_ref=lon_in.at[step, d], send_sem=halo_send.at[step, d],
                recv_sem=halo_recv.at[step, d], device_id=device, device_id_type=MESH,
            ))
        north = pltpu.make_async_remote_copy(
            src_ref=q.at[:, pl.ds(rows, HALO)], dst_ref=q.at[:, pl.ds(0, HALO)], send_sem=halo_send.at[step, 2],
            recv_sem=halo_recv.at[step, 2], device_id=(lon, jnp.minimum(lat + 1, 3)), device_id_type=MESH,
        )
        south = pltpu.make_async_remote_copy(
            src_ref=q.at[:, pl.ds(HALO, HALO)], dst_ref=q.at[:, pl.ds(rows + HALO, HALO)], send_sem=halo_send.at[step, 3],
            recv_sem=halo_recv.at[step, 3], device_id=(lon, jnp.maximum(lat - 1, 0)), device_id_type=MESH,
        )
        return copies, north, south

    def start_halos(q, step):
        copies, north, south = halo_copies(q, step)
        for copy in copies:
            copy.start()

        @pl.when(lat < 3)
        def _():
            north.start()

        @pl.when(lat > 0)
        def _():
            south.start()

    def wait_halos(q, step):
        copies, north, south = halo_copies(q, step)
        for copy in copies:
            copy.wait()

        @pl.when(lat < 3)
        def _():
            north.wait_send()
            south.wait_recv()

        @pl.when(lat > 0)
        def _():
            south.wait_send()
            north.wait_recv()

    blank = jnp.zeros((HALO, 128), jnp.float32)

    @pl.when(lat == 0)
    def _():
        for q in (q0, q1, q2):
            for n in range(q.shape[0]):
                q[n, pl.ds(0, HALO)] = blank

    @pl.when(lat == 3)
    def _():
        for q in (q0, q1, q2):
            for n in range(q.shape[0]):
                q[n, pl.ds(rows + HALO, HALO)] = blank

    loads[3].wait()

    def state_edges(n, carry):
        packed = blank
        for k in range(rows // 8):
            packed = edges(q0[n, pl.ds(HALO + 8 * k, 8)], packed, k)
        lon_out[0, n] = packed
        return carry

    lax.fori_loop(0, tracers * levels, state_edges, 0)
    start_halos(q0, 0)

    for copy in loads[4:]:
        copy.wait()

    def scale(n, carry):
        for b in range(rows // BLOCK):
            at = (n, pl.ds(b * BLOCK, BLOCK))
            sea = wet[at].astype(jnp.float32)
            diff[at] = diff[at] * sea
            zonal[at] = zonal[at] * sea * (1.0 / 12.0)
            merid[at] = merid[at] * sea * (1.0 / 12.0)
        return carry

    lax.fori_loop(0, levels, scale, 0)

    lanes = lax.broadcasted_iota(jnp.int32, (BLOCK, 128), 1)

    def stencil(q, step, n, level, b):
        start = HALO + b * BLOCK
        here = q[n, pl.ds(start, BLOCK)]
        beside = jnp.where(wide % 4 < 2, lon_in[step, 0, n], lon_in[step, 1, n])
        side = jnp.concatenate([roll(beside, 126 - 4 * (b * (BLOCK // 8) + k)) for k in range(BLOCK // 8)], axis=0)
        east_cell = roll(jnp.where(lanes == 0, side, here), 127)
        far_east = roll(jnp.where(lanes < 2, side, here), 126)
        west_cell = roll(jnp.where(lanes == 127, side, here), 1)
        far_west = roll(jnp.where(lanes >= 126, side, here), 2)
        north_cell = q[n, pl.ds(start + 1, BLOCK)]
        south_cell = q[n, pl.ds(start - 1, BLOCK)]
        far_north = q[n, pl.ds(start + 2, BLOCK)]
        far_south = q[n, pl.ds(start - 2, BLOCK)]
        at = (level, pl.ds(b * BLOCK, BLOCK))
        laplace = (east_cell + west_cell) + (north_cell + south_cell) - 4.0 * here
        along = 8.0 * (east_cell - west_cell) - (far_east - far_west)
        across = 8.0 * (north_cell - south_cell) - (far_north - far_south)
        return here + diff[at] * laplace - zonal[at] * along - merid[at] * across

    wait_halos(q0, 0)

    def first_step(n, carry):
        for b in range(rows // BLOCK):
            part[n, pl.ds(b * BLOCK, BLOCK)] = stencil(q0, 0, n, n % levels, b)
        return carry

    lax.fori_loop(0, tracers * levels, first_step, 0)

    def arrived(t, ref, back):
        a = ref.at[t, pl.ds(1, 127)] if t < tracers else ref.at[pl.ds(1, 127)]
        pltpu.make_async_copy(a, a, back.at[t]).wait()

    arrived(tracers, meta_in, recv_sem)
    rows_of = jnp.transpose(meta_in[:, 0, :])
    grid_row = lax.broadcasted_iota(jnp.int32, (rows, 128), 0).astype(jnp.float32)
    selector = jnp.concatenate(
        [jnp.where(grid_row == rows_of[s : s + 1], 1.0, 0.0).astype(jnp.bfloat16) for s in range(2)], axis=1
    )

    for t in range(tracers):
        arrived(t, recv, recv_sem)
        flat = recv.at[t].reshape(129 * 2 * levels, 128)

        def assemble(l, carry):
            data = jnp.concatenate([flat[pl.ds(s * levels + l, 128, stride=2 * levels), :] for s in range(2)], axis=0)
            high = data.astype(jnp.bfloat16)
            rest = data - high.astype(jnp.float32)
            middle = rest.astype(jnp.bfloat16)
            low = (rest - middle.astype(jnp.float32)).astype(jnp.bfloat16)
            total = jnp.dot(selector, low, preferred_element_type=jnp.float32)
            total += jnp.dot(selector, middle, preferred_element_type=jnp.float32)
            total += jnp.dot(selector, high, preferred_element_type=jnp.float32)
            n = t * levels + l
            packed = blank
            sea = wet[l].astype(jnp.float32)
            forcing = total * sea * (1.0 / STEPS)
            force[n] = forcing
            q1[n, pl.ds(HALO, rows)] = part[n] + forcing
            for k in range(rows // 8):
                packed = edges(q1[n, pl.ds(HALO + 8 * k, 8)], packed, k)
            lon_out[1, n] = packed
            return carry

        lax.fori_loop(0, levels, assemble, 0)

    start_halos(q1, 1)
    wait_halos(q1, 1)

    def second_step(n, carry):
        packed = blank
        for b in range(rows // BLOCK):
            fresh = stencil(q1, 1, n, n % levels, b) + force[n, pl.ds(b * BLOCK, BLOCK)]
            q2[n, pl.ds(HALO + b * BLOCK, BLOCK)] = fresh
            for k in range(BLOCK // 8):
                packed = edges(fresh[8 * k : 8 * k + 8], packed, b * (BLOCK // 8) + k)
        lon_out[2, n] = packed
        return carry

    lax.fori_loop(0, tracers * levels, second_step, 0)
    start_halos(q2, 2)
    wait_halos(q2, 2)

    def third_step(n, carry):
        for b in range(rows // BLOCK):
            part[n, pl.ds(b * BLOCK, BLOCK)] = (
                stencil(q2, 2, n, n % levels, b) + force[n, pl.ds(b * BLOCK, BLOCK)]
            )
        return carry

    lax.fori_loop(0, tracers * levels, third_step, 0)
    store = pltpu.make_async_copy(part, out, out_sem)
    store.start()
    store.wait()
    for t in range(tracers):
        arrived(t, send, send_sem)
    arrived(tracers, meta_out, send_sem)


def body(state, blocks, dest_tile, dest_row, kappa, lon_speed, lat_speed, sea_mask):
    tracers, levels, rows, columns = state.shape
    fields = tracers * levels
    tall = (fields, rows + 2 * HALO, columns)
    flat = (fields, rows, columns)
    f32, i32 = jnp.float32, jnp.int32
    anywhere = pl.BlockSpec(memory_space=pltpu.HBM)
    dma, vmem = pltpu.SemaphoreType.DMA, pltpu.VMEM
    result = pl.pallas_call(
        kernel,
        out_shape=jax.ShapeDtypeStruct(flat, f32),
        in_specs=[anywhere] * 8,
        out_specs=anywhere,
        scratch_shapes=[
            vmem((1, 128), i32), vmem((1, 128), i32),
            vmem(tall, f32), vmem(tall, f32), vmem(tall, f32), vmem(flat, f32), vmem(flat, f32),
            vmem(kappa.shape, f32), vmem(kappa.shape, f32), vmem(kappa.shape, f32), vmem(kappa.shape, i32),
            vmem((128, fields, columns), f32), vmem((8, 128), i32), pltpu.SMEM((8, 128), i32),
            vmem((128, 128), f32), vmem((128, 1, 128), f32), vmem((128, 1, 128), f32),
            vmem((tracers, 128, 2 * levels, columns), f32), vmem((tracers, 129, 2 * levels, columns), f32),
            vmem((STEPS, fields, 8, 128), f32), vmem((STEPS, 2, fields, 8, 128), f32),
            dma((8,)), dma, dma((tracers + 1,)), dma((tracers + 1,)),
            dma((STEPS, 4)), dma((STEPS, 4)), dma,
        ],
        compiler_params=pltpu.CompilerParams(
            collective_id=0, has_side_effects=True, vmem_limit_bytes=48 << 20
        ),
    )(
        state.reshape(flat), blocks.reshape(128, fields, columns), dest_tile.reshape(1, 128), dest_row.reshape(1, 128),
        kappa, lon_speed, lat_speed, sea_mask,
    )
    return result.reshape(state.shape)


def solution(mesh):
    placed = (
        P(None, None, "lat", "lon"),
        P(("lon", "lat"), None, None, None),
        P(("lon", "lat"), None),
        P(("lon", "lat")),
        P(None, "lat", "lon"),
        P(None, "lat", "lon"),
        P(None, "lat", "lon"),
        P(None, "lat", "lon"),
    )
    return jax.shard_map(
        body, mesh=mesh, in_specs=placed, out_specs=P(None, None, "lat", "lon"), check_vma=False
    )
```

```python
import jax
import jax.numpy as jnp
from jax import lax
from jax.experimental import pallas as pl
from jax.experimental.pallas import tpu as pltpu
from jax.sharding import PartitionSpec as P

MESH = pl.DeviceIdType.MESH
STEPS = 3
BANDS = 8
PARTNERS = 64
STRIDE = 27
SLOTS = 2
PIECE = 40
PAD = 8
EDGE = 2


def roll(x, amount):
    amount = amount % 128
    return x if amount == 0 else pltpu.roll(x, amount, 1)


def kernel(
    state, blocks, tile_at, row_at, kappa, lon_speed, lat_speed, mask, out,
    tile_ref, row_ref, held, table, table_s, plan, send, relay, recv,
    raw_state, raw_diff, raw_zonal, raw_merid, raw_wet, raw_force, scaled,
    q0, q1, q2, part, force, diff, zonal, merid, wet, lon_out, lon_in, lat_out, lat_in,
    load_sem, table_sem, core_send, core_recv, send_sem, recv_sem, halo_send, halo_recv, out_sem,
):
    levels, rows, columns = kappa.shape
    fields = state.shape[0]
    depth = rows // BANDS
    used = SLOTS * fields + 1
    lon, lat = lax.axis_index("lon"), lax.axis_index("lat")
    core = lat % 2
    me = lon * 2 + lat // 2
    other = (lon, lat + 1 - 2 * core)

    def partner(i):
        target = (me + i * STRIDE) % PARTNERS
        return (target // 2, (target % 2) * 2 + core)

    moves = (
        (tile_at, tile_ref), (row_at, row_ref), (blocks, held), (state, raw_state.at[pl.ds(0, fields)]),
        (kappa, raw_diff.at[pl.ds(0, levels)]), (lon_speed, raw_zonal.at[pl.ds(0, levels)]),
        (lat_speed, raw_merid.at[pl.ds(0, levels)]), (mask, raw_wet),
    )
    loads = [pltpu.make_async_copy(src, dst, load_sem.at[k]) for k, (src, dst) in enumerate(moves)]
    for copy in loads:
        copy.start()

    barrier = pltpu.get_barrier_semaphore()
    for device in (other, (lon, 3 - lat)):
        pl.semaphore_signal(barrier, inc=1, device_id=device, device_id_type=MESH)

    def greet(i, carry):
        pl.semaphore_signal(barrier, inc=1, device_id=partner(i), device_id_type=MESH)
        return carry

    lax.fori_loop(1, PARTNERS, greet, 0)
    loads[0].wait()
    loads[1].wait()

    tile_of = lax.broadcasted_iota(jnp.int32, (128, 128), 0)
    number = lax.broadcasted_iota(jnp.int32, (128, 128), 1)
    named = tile_ref[...] == tile_of
    first = jnp.min(jnp.where(named, number, 128), axis=1, keepdims=True)
    last = jnp.max(jnp.where(named, number, -1), axis=1, keepdims=True)
    row_f = row_ref[...].astype(jnp.float32)
    first_row = jnp.sum(jnp.where(number == first, row_f, 0.0), axis=1, keepdims=True)
    last_row = jnp.sum(jnp.where(number == last, row_f, 0.0), axis=1, keepdims=True)
    first_row = jnp.where(last >= 0, first_row, -1.0)
    last_row = jnp.where(last > first, last_row, -1.0)
    plan[...] = jnp.where(number == 0, first_row, last_row)
    slots = jnp.where(number == 0, jnp.minimum(first, 127), jnp.maximum(last, 0))
    table[...] = jnp.transpose(slots)[:8]
    to_scalars = pltpu.make_async_copy(table, table_s, table_sem)
    to_scalars.start()
    loads[2].wait()
    to_scalars.wait()

    def pack(i, carry):
        target = (me + i * STRIDE) % PARTNERS
        for h in range(2):
            tile = (target // 2) * 4 + (target % 2) * 2 + (core if h == 0 else 1 - core)
            for s in range(SLOTS):
                send[h, i, pl.ds(s * fields, fields)] = held[table_s[s, tile]]
            send[h, i, pl.ds(SLOTS * fields, 1)] = plan[pl.ds(tile, 1), :]
        return carry

    lax.fori_loop(0, PARTNERS, pack, 0)

    pl.semaphore_wait(barrier, PARTNERS + 1)
    across = pltpu.make_async_remote_copy(
        src_ref=send.at[1, :, pl.ds(0, used)], dst_ref=relay.at[:, pl.ds(0, used)],
        send_sem=core_send, recv_sem=core_recv, device_id=other, device_id_type=MESH,
    )
    across.start()

    def post(h):
        def one(i, carry):
            src = send.at[0, i] if h == 0 else relay.at[i]
            pltpu.make_async_remote_copy(
                src_ref=src.at[pl.ds(0, used)], dst_ref=recv.at[h * PARTNERS + i, pl.ds(0, used)],
                send_sem=send_sem.at[h], recv_sem=recv_sem.at[h], device_id=partner(i), device_id_type=MESH,
            ).start()
            return carry

        lax.fori_loop(1, PARTNERS, one, 0)

    post(0)
    recv[0] = send[0, 0]

    def turned(ref, r):
        flat = ref.reshape(ref.shape[0] * rows, columns)
        taken = []
        for b in range(BANDS):
            if ref.shape[0] > fields:
                taken.append(flat[pl.ds(b * depth + r, fields, stride=rows), :])
            else:
                level = flat[pl.ds(b * depth + r, levels, stride=rows), :]
                taken += [level] * (fields // levels)
        return jnp.transpose(jnp.concatenate(taken, axis=0))

    def sweep(count, unroll, step):
        def some(i, carry):
            for k in range(unroll):
                step(i * unroll + k)
            return carry

        lax.fori_loop(0, count // unroll, some, 0)

    inner = pl.ds(PAD, columns)
    loads[3].wait()

    def turn_state(r):
        q0[r + EDGE, inner] = turned(raw_state, r)

    sweep(depth, 4, turn_state)
    across.wait()
    recv[PARTNERS] = relay[0]
    post(1)

    east, west = ((lon + 1) % 32, lat), ((lon + 31) % 32, lat)
    lanes = lax.broadcasted_iota(jnp.int32, (8, 128), 1)
    width = 128 // BANDS
    many = columns // 8

    def halo_copies(step):
        def copy(src, dst, k, device):
            return pltpu.make_async_remote_copy(
                src_ref=src, dst_ref=dst, send_sem=halo_send.at[step, k], recv_sem=halo_recv.at[step, k],
                device_id=device, device_id_type=MESH,
            )

        return (
            copy(lon_out.at[step, 0], lon_in.at[step, 0], 0, east),
            copy(lon_out.at[step, 1], lon_in.at[step, 1], 1, west),
            copy(lat_out.at[step, 0], lat_in.at[step, 0], 2, (lon, jnp.minimum(lat + 1, 3))),
            copy(lat_out.at[step, 1], lat_in.at[step, 1], 3, (lon, jnp.maximum(lat - 1, 0))),
        )

    def start_halos(q, step):
        for k in range(EDGE):
            for half in range(2):
                up, down = jnp.zeros((8, 128), jnp.float32), jnp.zeros((8, 128), jnp.float32)
                for g in range(BANDS):
                    at = pl.ds(PAD + 8 * (half * BANDS + g), 8)
                    top, bottom = q[depth + k, at], q[EDGE + k, at]
                    q[k, at] = roll(top, width)
                    q[EDGE + depth + k, at] = roll(bottom, -width)
                    up = jnp.where(lanes // width == g, roll(top, width * (g + 1)), up)
                    down = jnp.where(lanes // width == g, roll(bottom, width * g), down)
                lat_out[step, 0, pl.ds(8 * (2 * k + half), 8)] = up
                lat_out[step, 1, pl.ds(8 * (2 * k + half), 8)] = down
        for r in range(depth):
            lon_out[step, 0, pl.ds(EDGE * r, EDGE)] = q[EDGE + r, pl.ds(PAD + columns - EDGE, EDGE)]
            lon_out[step, 1, pl.ds(EDGE * r, EDGE)] = q[EDGE + r, pl.ds(PAD, EDGE)]
        to_east, to_west, to_north, to_south = halo_copies(step)
        to_east.start()
        to_west.start()

        @pl.when(lat < 3)
        def _():
            to_north.start()

        @pl.when(lat > 0)
        def _():
            to_south.start()

    def wait_halos(q, step):
        to_east, to_west, to_north, to_south = halo_copies(step)
        to_east.wait()
        to_west.wait()

        @pl.when(lat < 3)
        def _():
            to_north.wait_send()
            to_south.wait_recv()

        @pl.when(lat > 0)
        def _():
            to_south.wait_send()
            to_north.wait_recv()

        for r in range(depth):
            q[EDGE + r, pl.ds(PAD - EDGE, EDGE)] = lon_in[step, 0, pl.ds(EDGE * r, EDGE)]
            q[EDGE + r, pl.ds(PAD + columns, EDGE)] = lon_in[step, 1, pl.ds(EDGE * r, EDGE)]
        for k in range(EDGE):
            for half in range(2):
                below = lat_in[step, 0, pl.ds(8 * (2 * k + half), 8)]
                above = lat_in[step, 1, pl.ds(8 * (2 * k + half), 8)]
                for g in range(BANDS):
                    at = pl.ds(PAD + 8 * (half * BANDS + g), 8)
                    q[k, at] = jnp.where(lanes < width, roll(below, -width * g), q[k, at])
                    n = EDGE + depth + k
                    q[n, at] = jnp.where(lanes >= 128 - width, roll(above, -width * (g + 1)), q[n, at])

    blank = jnp.zeros(lat_in.shape[2:], jnp.float32)
    for step in range(STEPS):

        @pl.when(lat == 0)
        def _():
            lat_in[step, 0] = blank

        @pl.when(lat == 3)
        def _():
            lat_in[step, 1] = blank

    start_halos(q0, 0)

    for copy in loads[4:]:
        copy.wait()

    def scale(n, carry):
        for b in range(rows // 32):
            at = (n, pl.ds(b * 32, 32))
            sea = raw_wet[at].astype(jnp.float32)
            raw_diff[at] = raw_diff[at] * sea
            raw_zonal[at] = raw_zonal[at] * sea * (1.0 / 12.0)
            raw_merid[at] = raw_merid[at] * sea * (1.0 / 12.0)
            scaled[at] = sea * (1.0 / STEPS)
        return carry

    lax.fori_loop(0, levels, scale, 0)
    for raw, ref in ((raw_diff, diff), (raw_zonal, zonal), (raw_merid, merid), (scaled, wet)):

        def turn(r):
            ref[r] = turned(raw, r)

        sweep(depth, 4, turn)

    def stencil(q, r, start, size):
        n, here_at = r + EDGE, pl.ds(PAD + start, size)
        here = q[n, here_at]
        east_cell, west_cell = q[n, pl.ds(PAD + start + 1, size)], q[n, pl.ds(PAD + start - 1, size)]
        far_east, far_west = q[n, pl.ds(PAD + start + 2, size)], q[n, pl.ds(PAD + start - 2, size)]
        north_cell, south_cell = q[n + 1, here_at], q[n - 1, here_at]
        far_north, far_south = q[n + 2, here_at], q[n - 2, here_at]
        at = (r, pl.ds(start, size))
        laplace = (east_cell + west_cell) + (north_cell + south_cell) - 4.0 * here
        along = 8.0 * (east_cell - west_cell) - (far_east - far_west)
        across = 8.0 * (north_cell - south_cell) - (far_north - far_south)
        return here + diff[at] * laplace - zonal[at] * along - merid[at] * across

    whole = [(32 * b, 32) for b in range(columns // 32)]
    middle = [(8, 32), (40, 32), (72, 32), (104, 16)]
    ends = [(0, 8), (columns - 8, 8)]

    wait_halos(q0, 0)

    def first_step(r):
        for start, size in whole:
            part[r, pl.ds(start, size)] = stencil(q0, r, start, size)

    sweep(depth, 2, first_step)

    for h in range(2):
        a = recv.at[pl.ds(h * PARTNERS + 1, PARTNERS - 1), pl.ds(0, used)]
        pltpu.make_async_copy(a, a, recv_sem.at[h]).wait()
    flat = recv.reshape(recv.shape[0] * PIECE, columns)
    rows_of = jnp.transpose(flat[pl.ds(SLOTS * fields, 128, stride=PIECE), :])
    grid_row = lax.broadcasted_iota(jnp.int32, (rows, 128), 0).astype(jnp.float32)
    selector = jnp.concatenate(
        [jnp.where(grid_row == rows_of[s : s + 1], 1.0, 0.0).astype(jnp.bfloat16) for s in range(SLOTS)], axis=1
    )

    def assemble(n):
        data = jnp.concatenate([flat[pl.ds(s * fields + n, 128, stride=PIECE), :] for s in range(SLOTS)], axis=0)
        high = data.astype(jnp.bfloat16)
        rest = (data - high.astype(jnp.float32)).astype(jnp.bfloat16)
        both = jnp.dot(selector, jnp.concatenate([high, rest], axis=1), preferred_element_type=jnp.float32)
        raw_force[n] = both[:, :columns] + both[:, columns:]

    sweep(fields, 2, assemble)

    def add_forcing(r):
        forcing = turned(raw_force, r) * wet[r]
        force[r] = forcing
        q1[r + EDGE, inner] = part[r] + forcing

    sweep(depth, 4, add_forcing)

    def advance(q, r, start, size):
        return stencil(q, r, start, size) + force[r, pl.ds(start, size)]

    start_halos(q1, 1)

    def second_inside(r):
        for start, size in middle:
            q2[r + 2 * EDGE, pl.ds(PAD + start, size)] = advance(q1, r + EDGE, start, size)

    sweep(depth - 2 * EDGE, 2, second_inside)
    wait_halos(q1, 1)

    def second_ends(r):
        for start, size in ends:
            q2[r + 2 * EDGE, pl.ds(PAD + start, size)] = advance(q1, r + EDGE, start, size)

    sweep(depth - 2 * EDGE, 4, second_ends)
    for r in (0, 1, depth - 2, depth - 1):
        for start, size in whole:
            q2[r + EDGE, pl.ds(PAD + start, size)] = advance(q1, r, start, size)

    start_halos(q2, 2)

    def third_inside(r):
        for start, size in middle:
            part[r + EDGE, pl.ds(start, size)] = advance(q2, r + EDGE, start, size)

    sweep(depth - 2 * EDGE, 2, third_inside)
    wait_halos(q2, 2)
    result = raw_state.reshape(raw_state.shape[0] * rows, columns)

    def finish(r, spans):
        for start, size in spans:
            part[r, pl.ds(start, size)] = advance(q2, r, start, size)
        back = jnp.transpose(part[r])
        for b in range(BANDS):
            result[pl.ds(b * depth + r, fields, stride=rows), :] = back[b * fields : (b + 1) * fields]

    sweep(depth - 2 * EDGE, 4, lambda r: finish(r + EDGE, ends))
    for r in (0, 1, depth - 2, depth - 1):
        finish(r, whole)
    store = pltpu.make_async_copy(raw_state.at[pl.ds(0, fields)], out, out_sem)
    store.start()
    for h in range(2):
        a = recv.at[pl.ds(h * PARTNERS + 1, PARTNERS - 1), pl.ds(0, used)]
        pltpu.make_async_copy(a, a, send_sem.at[h]).wait()
    store.wait()


def body(state, blocks, dest_tile, dest_row, kappa, lon_speed, lat_speed, sea_mask):
    tracers, levels, rows, columns = state.shape
    fields, depth = tracers * levels, rows // BANDS
    flat = (fields, rows, columns)
    f32, i32 = jnp.float32, jnp.int32
    anywhere = pl.BlockSpec(memory_space=pltpu.HBM)
    dma, vmem = pltpu.SemaphoreType.DMA, pltpu.VMEM
    tall = vmem((depth + 2 * EDGE, columns + 2 * PAD, 128), f32)
    turned = vmem((depth, columns, 128), f32)
    raw, coarse = vmem((fields + 1, rows, columns), f32), vmem((levels + 1, rows, columns), f32)
    result = pl.pallas_call(
        kernel,
        out_shape=jax.ShapeDtypeStruct(flat, f32),
        in_specs=[anywhere] * 8,
        out_specs=anywhere,
        scratch_shapes=[
            vmem((1, 128), i32), vmem((1, 128), i32), vmem((128, fields, columns), f32),
            vmem((8, 128), i32), pltpu.SMEM((8, 128), i32), vmem((128, 128), f32),
            vmem((2, PARTNERS, PIECE, columns), f32), vmem((PARTNERS, PIECE, columns), f32),
            vmem((2 * PARTNERS + 1, PIECE, columns), f32),
            raw, coarse, coarse, coarse, vmem((levels, rows, columns), i32), raw, coarse,
            tall, tall, tall, turned, turned, turned, turned, turned, turned,
            vmem((STEPS, 2, EDGE * depth, 128), f32), vmem((STEPS, 2, EDGE * depth, 128), f32),
            vmem((STEPS, 2, 16 * EDGE, 128), f32), vmem((STEPS, 2, 16 * EDGE, 128), f32),
            dma((8,)), dma, dma, dma, dma((2,)), dma((2,)), dma((STEPS, 4)), dma((STEPS, 4)), dma,
        ],
        compiler_params=pltpu.CompilerParams(
            collective_id=0, has_side_effects=True, vmem_limit_bytes=63 << 20
        ),
    )(
        state.reshape(flat), blocks.reshape(128, fields, columns), dest_tile.reshape(1, 128), dest_row.reshape(1, 128),
        kappa, lon_speed, lat_speed, sea_mask,
    )
    return result.reshape(state.shape)


def solution(mesh):
    placed = (
        P(None, None, "lat", "lon"),
        P(("lon", "lat"), None, None, None),
        P(("lon", "lat"), None),
        P(("lon", "lat")),
        P(None, "lat", "lon"),
        P(None, "lat", "lon"),
        P(None, "lat", "lon"),
        P(None, "lat", "lon"),
    )
    return jax.shard_map(
        body, mesh=mesh, in_specs=placed, out_specs=P(None, None, "lat", "lon"), check_vma=False
    )
```

```python
import jax
import jax.numpy as jnp
from jax import lax
from jax.experimental import pallas as pl
from jax.experimental.pallas import tpu as pltpu
from jax.sharding import PartitionSpec as P

MESH = pl.DeviceIdType.MESH
STEPS = 3
BANDS = 8
PARTNERS = 64
SLOTS = 2
PIECE = 40
VL = 44
PAD = 8
EDGE = 2
OFFSETS = sorted(
    ((z, x, y) for z in range(4) for x in range(4) for y in range(4)),
    key=lambda o: (sum(d > 0 for d in o), (5 * o[0] + 11 * o[1] + 7 * o[2]) % 13),
)
LINES, PLANES = 10, 37


def roll(x, amount):
    amount = amount % 128
    return x if amount == 0 else pltpu.roll(x, amount, 1)


def kernel(
    state, blocks, tile_at, row_at, kappa, lon_speed, lat_speed, mask, part,
    tile_ref, row_ref, held, table, table_s, plan, send, relay, recv,
    raw_state, raw_diff, raw_zonal, raw_merid, raw_wet, raw_force, scaled,
    q0, q1, q2, force, diff, zonal, merid, wet, lon_out, lon_in, lat_out, lat_in,
    load_sem, table_sem, line_sem, core_send, core_recv, send_sem, recv_sem, halo_send, halo_recv,
):
    levels, rows, columns = kappa.shape
    fields = state.shape[0]
    depth = rows // BANDS
    used = SLOTS * fields + 1
    lon, lat = lax.axis_index("lon"), lax.axis_index("lat")
    core = lat % 2
    z, x, y = lon // 8, (lat // 2) * 2 + (lon // 4) % 2, lon % 4
    other = (lon, lat + 1 - 2 * core)

    def place(i):
        dz, dx, dy = OFFSETS[i]
        return (z + dz) % 4, (x + dx) % 4, (y + dy) % 4

    def partner(i):
        z, x, y = place(i)
        return (z * 8 + (x % 2) * 4 + y, (x // 2) * 2 + core)

    moves = (
        (tile_at, tile_ref), (row_at, row_ref), (blocks, held), (state, raw_state.at[pl.ds(0, fields)]),
        (kappa, raw_diff.at[pl.ds(0, levels)]), (lon_speed, raw_zonal.at[pl.ds(0, levels)]),
        (lat_speed, raw_merid.at[pl.ds(0, levels)]), (mask, raw_wet),
    )
    loads = [pltpu.make_async_copy(src, dst, load_sem.at[k]) for k, (src, dst) in enumerate(moves)]
    for copy in loads:
        copy.start()

    barrier = pltpu.get_barrier_semaphore()
    for device in [partner(i) for i in range(1, LINES)] + [other, (lon, 3 - lat)]:
        pl.semaphore_signal(barrier, inc=1, device_id=device, device_id_type=MESH)
    loads[0].wait()
    loads[1].wait()

    tile_of = lax.broadcasted_iota(jnp.int32, (128, 128), 0)
    number = lax.broadcasted_iota(jnp.int32, (128, 128), 1)
    named = tile_ref[...] == tile_of
    first = jnp.min(jnp.where(named, number, 128), axis=1, keepdims=True)
    last = jnp.max(jnp.where(named, number, -1), axis=1, keepdims=True)
    row_f = row_ref[...].astype(jnp.float32)
    first_row = jnp.sum(jnp.where(number == first, row_f, 0.0), axis=1, keepdims=True)
    last_row = jnp.sum(jnp.where(number == last, row_f, 0.0), axis=1, keepdims=True)
    first_row = jnp.where(last >= 0, first_row, -1.0)
    last_row = jnp.where(last > first, last_row, -1.0)
    plan[...] = jnp.where(number == 0, first_row, last_row)
    slots = jnp.where(number == 0, jnp.minimum(first, 127), jnp.maximum(last, 0))
    table[...] = jnp.transpose(slots)[:8]
    to_scalars = pltpu.make_async_copy(table, table_s, table_sem)
    to_scalars.start()
    loads[2].wait()
    to_scalars.wait()

    for i in range(PARTNERS):
        tz, tx, ty = place(i)
        for h in range(2):
            tile = tz * 32 + (tx % 2) * 16 + ty * 4 + (tx // 2) * 2 + (core if h == 0 else 1 - core)
            for s in range(SLOTS):
                send[h, i, pl.ds(s * fields, fields)] = held[table_s[s, tile]]
            send[h, i, pl.ds(SLOTS * fields, 1)] = plan[pl.ds(tile, 1), :]

    across = pltpu.make_async_remote_copy(
        src_ref=send.at[1, :, pl.ds(0, used)], dst_ref=relay.at[:, pl.ds(0, used)],
        send_sem=core_send, recv_sem=core_recv, device_id=other, device_id_type=MESH,
    )

    def post(h, numbers):
        for i in numbers:
            src = send.at[0, i] if h == 0 else relay.at[i]
            pltpu.make_async_remote_copy(
                src_ref=src.at[pl.ds(0, used)], dst_ref=recv.at[h * PARTNERS + i, pl.ds(0, used)],
                send_sem=send_sem.at[h], recv_sem=recv_sem.at[h], device_id=partner(i), device_id_type=MESH,
            ).start()

    pl.semaphore_wait(barrier, LINES + 1)
    for i in range(1, LINES):
        pl.semaphore_signal(line_sem.at[0], inc=1, device_id=partner(i), device_id_type=MESH)
    across.start()
    post(0, range(1, LINES))
    recv[0] = send[0, 0]
    pl.semaphore_wait(line_sem.at[0], LINES - 1)
    for i in range(1, LINES):
        pl.semaphore_signal(line_sem.at[1], inc=1, device_id=partner(i), device_id_type=MESH)
    post(0, range(LINES, PLANES))
    across.wait()
    recv[PARTNERS] = relay[0]
    post(1, range(1, PLANES))
    pl.semaphore_wait(line_sem.at[1], LINES - 1)
    post(0, range(PLANES, PARTNERS))
    post(1, range(PLANES, PARTNERS))

    def turned(ref, r):
        flat = ref.reshape(ref.shape[0] * rows, columns)
        taken = []
        for b in range(BANDS):
            if ref.shape[0] > fields:
                taken.append(flat[pl.ds(b * depth + r, fields, stride=rows), :])
            else:
                level = flat[pl.ds(b * depth + r, levels, stride=rows), :]
                taken += [level] * (fields // levels)
        return jnp.transpose(jnp.concatenate(taken, axis=0))

    def sweep(count, unroll, step):
        def some(i, carry):
            for k in range(unroll):
                step(i * unroll + k)
            return carry

        lax.fori_loop(0, count // unroll, some, 0)

    inner = pl.ds(PAD, columns)
    loads[3].wait()

    def turn_state(r):
        q0[r + EDGE, inner] = turned(raw_state, r)

    sweep(depth, 4, turn_state)

    east, west = ((lon + 1) % 32, lat), ((lon + 31) % 32, lat)
    lanes = lax.broadcasted_iota(jnp.int32, (8, 128), 1)
    width = 128 // BANDS
    many = columns // 8

    def halo_copies(step):
        def copy(src, dst, k, device):
            return pltpu.make_async_remote_copy(
                src_ref=src, dst_ref=dst, send_sem=halo_send.at[step, k], recv_sem=halo_recv.at[step, k],
                device_id=device, device_id_type=MESH,
            )

        return (
            copy(lon_out.at[step, 0], lon_in.at[step, 0], 0, east),
            copy(lon_out.at[step, 1], lon_in.at[step, 1], 1, west),
            copy(lat_out.at[step, 0], lat_in.at[step, 0], 2, (lon, jnp.minimum(lat + 1, 3))),
            copy(lat_out.at[step, 1], lat_in.at[step, 1], 3, (lon, jnp.maximum(lat - 1, 0))),
        )

    def start_halos(q, step):
        to_east, to_west, to_north, to_south = halo_copies(step)
        for r in range(depth):
            lon_out[step, 0, pl.ds(EDGE * r, EDGE)] = q[EDGE + r, pl.ds(PAD + columns - EDGE, EDGE)]
            lon_out[step, 1, pl.ds(EDGE * r, EDGE)] = q[EDGE + r, pl.ds(PAD, EDGE)]
        to_east.start()
        to_west.start()
        for k in range(EDGE):
            for half in range(2):
                up, down = jnp.zeros((8, 128), jnp.float32), jnp.zeros((8, 128), jnp.float32)
                for g in range(BANDS):
                    at = pl.ds(PAD + 8 * (half * BANDS + g), 8)
                    top, bottom = q[depth + k, at], q[EDGE + k, at]
                    q[k, at] = roll(top, width)
                    q[EDGE + depth + k, at] = roll(bottom, -width)
                    up = jnp.where(lanes // width == g, roll(top, width * (g + 1)), up)
                    down = jnp.where(lanes // width == g, roll(bottom, width * g), down)
                lat_out[step, 0, pl.ds(8 * (2 * k + half), 8)] = up
                lat_out[step, 1, pl.ds(8 * (2 * k + half), 8)] = down

        @pl.when(lat < 3)
        def _():
            to_north.start()

        @pl.when(lat > 0)
        def _():
            to_south.start()

    def wait_halos(q, step):
        to_east, to_west, to_north, to_south = halo_copies(step)
        to_east.wait()
        to_west.wait()

        @pl.when(lat < 3)
        def _():
            to_north.wait_send()
            to_south.wait_recv()

        @pl.when(lat > 0)
        def _():
            to_south.wait_send()
            to_north.wait_recv()

        for r in range(depth):
            q[EDGE + r, pl.ds(PAD - EDGE, EDGE)] = lon_in[step, 0, pl.ds(EDGE * r, EDGE)]
            q[EDGE + r, pl.ds(PAD + columns, EDGE)] = lon_in[step, 1, pl.ds(EDGE * r, EDGE)]
        for k in range(EDGE):
            for half in range(2):
                below = lat_in[step, 0, pl.ds(8 * (2 * k + half), 8)]
                above = lat_in[step, 1, pl.ds(8 * (2 * k + half), 8)]
                for g in range(BANDS):
                    at = pl.ds(PAD + 8 * (half * BANDS + g), 8)
                    q[k, at] = jnp.where(lanes < width, roll(below, -width * g), q[k, at])
                    n = EDGE + depth + k
                    q[n, at] = jnp.where(lanes >= 128 - width, roll(above, -width * (g + 1)), q[n, at])

    blank = jnp.zeros(lat_in.shape[2:], jnp.float32)
    for step in range(STEPS):

        @pl.when(lat == 0)
        def _():
            lat_in[step, 0] = blank

        @pl.when(lat == 3)
        def _():
            lat_in[step, 1] = blank

    start_halos(q0, 0)

    for copy in loads[4:]:
        copy.wait()

    def scale(n, carry):
        for b in range(rows // 32):
            at = (n, pl.ds(b * 32, 32))
            sea = raw_wet[at].astype(jnp.float32)
            raw_diff[at] = raw_diff[at] * sea
            raw_zonal[at] = raw_zonal[at] * sea * (1.0 / 12.0)
            raw_merid[at] = raw_merid[at] * sea * (1.0 / 12.0)
            scaled[at] = sea * (1.0 / STEPS)
        return carry

    lax.fori_loop(0, levels, scale, 0)
    for raw, ref in ((raw_diff, diff), (raw_zonal, zonal), (raw_merid, merid), (scaled, wet)):

        def turn(r):
            ref[r] = turned(raw, r)

        sweep(depth, 4, turn)

    def stencil(q, r, start, size):
        n, here_at = r + EDGE, pl.ds(PAD + start, size)
        here = q[n, here_at]
        east_cell, west_cell = q[n, pl.ds(PAD + start + 1, size)], q[n, pl.ds(PAD + start - 1, size)]
        far_east, far_west = q[n, pl.ds(PAD + start + 2, size)], q[n, pl.ds(PAD + start - 2, size)]
        north_cell, south_cell = q[n + 1, here_at], q[n - 1, here_at]
        far_north, far_south = q[n + 2, here_at], q[n - 2, here_at]
        at = (r, pl.ds(start, size))
        laplace = (east_cell + west_cell) + (north_cell + south_cell) - 4.0 * here
        along = 8.0 * (east_cell - west_cell) - (far_east - far_west)
        across = 8.0 * (north_cell - south_cell) - (far_north - far_south)
        return here + diff[at] * laplace - zonal[at] * along - merid[at] * across

    whole = [(32 * b, 32) for b in range(columns // 32)]
    middle = [(8, 32), (40, 32), (72, 32), (104, 16)]
    ends = [(0, 8), (columns - 8, 8)]

    wait_halos(q0, 0)

    def first_step(r):
        for start, size in whole:
            part[r, pl.ds(start, size)] = stencil(q0, r, start, size)

    sweep(depth, 2, first_step)

    for h in range(2):
        a = recv.at[pl.ds(h * PARTNERS + 1, PARTNERS - 1), pl.ds(0, used)]
        pltpu.make_async_copy(a, a, recv_sem.at[h]).wait()
    flat = recv.reshape(recv.shape[0] * PIECE, columns)
    rows_of = jnp.transpose(flat[pl.ds(SLOTS * fields, 128, stride=PIECE), :])
    grid_row = lax.broadcasted_iota(jnp.int32, (rows, 128), 0).astype(jnp.float32)
    selector = jnp.concatenate(
        [jnp.where(grid_row == rows_of[s : s + 1], 1.0, 0.0).astype(jnp.bfloat16) for s in range(SLOTS)], axis=1
    )

    def assemble(n):
        data = jnp.concatenate([flat[pl.ds(s * fields + n, 128, stride=PIECE), :] for s in range(SLOTS)], axis=0)
        high = data.astype(jnp.bfloat16)
        rest = (data - high.astype(jnp.float32)).astype(jnp.bfloat16)
        both = jnp.dot(selector, jnp.concatenate([high, rest], axis=1), preferred_element_type=jnp.float32)
        raw_force[n] = both[:, :columns] + both[:, columns:]

    sweep(fields, 2, assemble)

    def add_forcing(r):
        forcing = turned(raw_force, r) * wet[r]
        force[r] = forcing
        q1[r + EDGE, inner] = part[r] + forcing

    sweep(depth, 4, add_forcing)

    def advance(q, r, start, size):
        return stencil(q, r, start, size) + force[r, pl.ds(start, size)]

    start_halos(q1, 1)

    def second_inside(r):
        for start, size in middle:
            q2[r + 2 * EDGE, pl.ds(PAD + start, size)] = advance(q1, r + EDGE, start, size)

    sweep(depth - 2 * EDGE, 2, second_inside)
    wait_halos(q1, 1)

    def second_ends(r):
        for start, size in ends:
            q2[r + 2 * EDGE, pl.ds(PAD + start, size)] = advance(q1, r + EDGE, start, size)

    sweep(depth - 2 * EDGE, 4, second_ends)
    for r in (0, 1, depth - 2, depth - 1):
        for start, size in whole:
            q2[r + EDGE, pl.ds(PAD + start, size)] = advance(q1, r, start, size)

    start_halos(q2, 2)

    def third_inside(r):
        for start, size in middle:
            part[r + EDGE, pl.ds(start, size)] = advance(q2, r + EDGE, start, size)

    sweep(depth - 2 * EDGE, 2, third_inside)
    wait_halos(q2, 2)

    def third_ends(r):
        for start, size in ends:
            part[r + EDGE, pl.ds(start, size)] = advance(q2, r + EDGE, start, size)

    sweep(depth - 2 * EDGE, 4, third_ends)
    for r in (0, 1, depth - 2, depth - 1):
        for start, size in whole:
            part[r, pl.ds(start, size)] = advance(q2, r, start, size)
    for h in range(2):
        a = recv.at[pl.ds(h * PARTNERS + 1, PARTNERS - 1), pl.ds(0, used)]
        pltpu.make_async_copy(a, a, send_sem.at[h]).wait()


def turn_back(bands, out, result, out_sem):
    fields, _, depth, columns = out.shape
    flat = result.reshape((fields + 1) * BANDS * depth, columns)
    copies = []
    for group in range(depth // 8):
        for r in range(group * 8, group * 8 + 8):
            back = jnp.transpose(bands[r])
            for b in range(BANDS):
                flat[pl.ds(b * depth + r, fields, stride=BANDS * depth), :] = back[b * fields : (b + 1) * fields]
        rows = pl.ds(group * 8, 8)
        copy = pltpu.make_async_copy(
            result.at[pl.ds(0, fields), :, rows], out.at[:, :, rows], out_sem.at[group]
        )
        copy.start()
        copies.append(copy)
    for copy in copies:
        copy.wait()


def body(state, blocks, dest_tile, dest_row, kappa, lon_speed, lat_speed, sea_mask):
    tracers, levels, rows, columns = state.shape
    fields, depth = tracers * levels, rows // BANDS
    flat = (fields, rows, columns)
    f32, i32 = jnp.float32, jnp.int32
    anywhere = pl.BlockSpec(memory_space=pltpu.HBM)
    dma, vmem = pltpu.SemaphoreType.DMA, pltpu.VMEM
    tall = vmem((depth + 2 * EDGE, columns + 2 * PAD, 128), f32)
    turned = vmem((depth, columns, 128), f32)
    raw, coarse = vmem((fields + 1, rows, columns), f32), vmem((levels + 1, rows, columns), f32)
    bands = pl.pallas_call(
        kernel,
        out_shape=jax.ShapeDtypeStruct((depth, columns, 128), f32),
        in_specs=[anywhere] * 8,
        out_specs=pl.BlockSpec(memory_space=pltpu.VMEM),
        scratch_shapes=[
            vmem((1, 128), i32), vmem((1, 128), i32), vmem((128, fields, columns), f32),
            vmem((8, 128), i32), pltpu.SMEM((8, 128), i32), vmem((128, 128), f32),
            vmem((2, PARTNERS, PIECE, columns), f32), vmem((PARTNERS, PIECE, columns), f32),
            vmem((2 * PARTNERS + 1, PIECE, columns), f32),
            raw, coarse, coarse, coarse, vmem((levels, rows, columns), i32), raw, coarse,
            tall, tall, tall, turned, turned, turned, turned, turned,
            vmem((STEPS, 2, EDGE * depth, 128), f32), vmem((STEPS, 2, EDGE * depth, 128), f32),
            vmem((STEPS, 2, 16 * EDGE, 128), f32), vmem((STEPS, 2, 16 * EDGE, 128), f32),
            dma((8,)), dma, pltpu.SemaphoreType.REGULAR((2,)), dma, dma, dma((2,)), dma((2,)), dma((STEPS, 4)), dma((STEPS, 4)),
        ],
        compiler_params=pltpu.CompilerParams(
            collective_id=0, has_side_effects=True, vmem_limit_bytes=VL << 20
        ),
    )(*[
        pltpu.with_memory_space_constraint(x, pltpu.HBM)
        for x in (
            state.reshape(flat), blocks.reshape(128, fields, columns), dest_tile.reshape(1, 128),
            dest_row.reshape(1, 128), kappa, lon_speed, lat_speed, sea_mask,
        )
    ])
    result = pl.pallas_call(
        turn_back,
        out_shape=jax.ShapeDtypeStruct((fields, BANDS, depth, columns), f32),
        in_specs=[pl.BlockSpec(memory_space=pltpu.VMEM)],
        out_specs=anywhere,
        scratch_shapes=[vmem((fields + 1, BANDS, depth, columns), f32), dma((depth // 8,))],
        compiler_params=pltpu.CompilerParams(vmem_limit_bytes=16 << 20),
    )(bands)
    return result.reshape(state.shape)


def solution(mesh):
    placed = (
        P(None, None, "lat", "lon"),
        P(("lon", "lat"), None, None, None),
        P(("lon", "lat"), None),
        P(("lon", "lat")),
        P(None, "lat", "lon"),
        P(None, "lat", "lon"),
        P(None, "lat", "lon"),
        P(None, "lat", "lon"),
    )
    return jax.shard_map(
        body, mesh=mesh, in_specs=placed, out_specs=P(None, None, "lat", "lon"), check_vma=False
    )
```

```python
import jax
import jax.numpy as jnp
from jax import lax
from jax.experimental import pallas as pl
from jax.experimental.pallas import tpu as pltpu
from jax.sharding import PartitionSpec as P

MESH = pl.DeviceIdType.MESH
STEPS = 3
BANDS = 8
PARTNERS = 64
SLOTS = 2
PIECE = 40
VL = 44
PAD = 8
EDGE = 2
OFFSETS = sorted(
    ((z, x, y) for z in range(4) for x in range(4) for y in range(4)),
    key=lambda o: (sum(d > 0 for d in o), -sum(d == 2 for d in o), (5 * o[0] + 11 * o[1] + 7 * o[2]) % 13),
)
LINES, PLANES = 10, 37


def roll(x, amount):
    amount = amount % 128
    return x if amount == 0 else pltpu.roll(x, amount, 1)


def kernel(
    state, blocks, tile_at, row_at, kappa, lon_speed, lat_speed, mask, part,
    tile_ref, row_ref, held, table, table_s, plan, send, relay, recv,
    raw_state, raw_diff, raw_zonal, raw_merid, raw_wet, raw_force, scaled,
    q0, q1, q2, force, diff, zonal, merid, wet, lon_out, lon_in, lat_out, lat_in,
    load_sem, table_sem, line_sem, core_send, core_recv, send_sem, recv_sem, halo_send, halo_recv,
):
    levels, rows, columns = kappa.shape
    fields = state.shape[0]
    depth = rows // BANDS
    used = SLOTS * fields + 1
    lon, lat = lax.axis_index("lon"), lax.axis_index("lat")
    core = lat % 2
    z, x, y = lon // 8, (lat // 2) * 2 + (lon // 4) % 2, lon % 4
    other = (lon, lat + 1 - 2 * core)

    def place(i):
        dz, dx, dy = OFFSETS[i]
        return (z + dz) % 4, (x + dx) % 4, (y + dy) % 4

    def partner(i):
        z, x, y = place(i)
        return (z * 8 + (x % 2) * 4 + y, (x // 2) * 2 + core)

    moves = (
        (tile_at, tile_ref), (row_at, row_ref), (blocks, held), (state, raw_state.at[pl.ds(0, fields)]),
        (kappa, raw_diff.at[pl.ds(0, levels)]), (lon_speed, raw_zonal.at[pl.ds(0, levels)]),
        (lat_speed, raw_merid.at[pl.ds(0, levels)]), (mask, raw_wet),
    )
    loads = [pltpu.make_async_copy(src, dst, load_sem.at[k]) for k, (src, dst) in enumerate(moves)]
    for copy in loads[:4]:
        copy.start()
    east, west = ((lon + 1) % 32, lat), ((lon + 31) % 32, lat)

    barrier = pltpu.get_barrier_semaphore()
    for device in [partner(i) for i in range(1, LINES)] + [other, (lon, 3 - lat), east, west]:
        pl.semaphore_signal(barrier, inc=1, device_id=device, device_id_type=MESH)
    loads[0].wait()
    loads[1].wait()

    tile_of = lax.broadcasted_iota(jnp.int32, (128, 128), 0)
    number = lax.broadcasted_iota(jnp.int32, (128, 128), 1)
    named = tile_ref[...] == tile_of
    first = jnp.min(jnp.where(named, number, 128), axis=1, keepdims=True)
    last = jnp.max(jnp.where(named, number, -1), axis=1, keepdims=True)
    row_f = row_ref[...].astype(jnp.float32)
    first_row = jnp.sum(jnp.where(number == first, row_f, 0.0), axis=1, keepdims=True)
    last_row = jnp.sum(jnp.where(number == last, row_f, 0.0), axis=1, keepdims=True)
    first_row = jnp.where(last >= 0, first_row, -1.0)
    last_row = jnp.where(last > first, last_row, -1.0)
    plan[...] = jnp.where(number == 0, first_row, last_row)
    slots = jnp.where(number == 0, jnp.minimum(first, 127), jnp.maximum(last, 0))
    table[...] = jnp.transpose(slots)[:8]
    to_scalars = pltpu.make_async_copy(table, table_s, table_sem)
    to_scalars.start()
    loads[2].wait()
    to_scalars.wait()

    def pack(h, numbers):
        for i in numbers:
            tz, tx, ty = place(i)
            tile = tz * 32 + (tx % 2) * 16 + ty * 4 + (tx // 2) * 2 + (core if h == 0 else 1 - core)
            for s in range(SLOTS):
                send[h, i, pl.ds(s * fields, fields)] = held[table_s[s, tile]]
            send[h, i, pl.ds(SLOTS * fields, 1)] = plan[pl.ds(tile, 1), :]

    pack(1, range(PARTNERS))
    pack(0, range(PARTNERS))

    def turned(ref, r):
        flat = ref.reshape(ref.shape[0] * rows, columns)
        count = ref.shape[0] - 1
        taken = [flat[pl.ds(n * rows + r, BANDS, stride=depth), :] for n in range(count)]
        return jnp.transpose(jnp.concatenate(taken * (fields // count), axis=0))

    def sweep(count, unroll, step):
        def some(i, carry):
            for k in range(unroll):
                step(i * unroll + k)
            return carry

        lax.fori_loop(0, count // unroll, some, 0)

    inner = pl.ds(PAD, columns)

    lanes = lax.broadcasted_iota(jnp.int32, (8, 128), 1)

    def halo_copies(step):
        def copy(src, dst, k, device):
            return pltpu.make_async_remote_copy(
                src_ref=src, dst_ref=dst, send_sem=halo_send.at[step, k], recv_sem=halo_recv.at[step, k],
                device_id=device, device_id_type=MESH,
            )

        return (
            copy(lon_out.at[step, 0], lon_in.at[step, 0], 0, east),
            copy(lon_out.at[step, 1], lon_in.at[step, 1], 1, west),
            copy(lat_out.at[step, 0], lat_in.at[step, 0], 2, (lon, jnp.minimum(lat + 1, 3))),
            copy(lat_out.at[step, 1], lat_in.at[step, 1], 3, (lon, jnp.maximum(lat - 1, 0))),
        )

    def start_halos(q, step, now=True):
        to_east, to_west, to_north, to_south = halo_copies(step)
        for r in range(depth):
            lon_out[step, 0, pl.ds(EDGE * r, EDGE)] = q[EDGE + r, pl.ds(PAD + columns - EDGE, EDGE)]
            lon_out[step, 1, pl.ds(EDGE * r, EDGE)] = q[EDGE + r, pl.ds(PAD, EDGE)]
        if now:
            to_east.start()
            to_west.start()
        for k in range(EDGE):
            for half in range(2):
                up, down = jnp.zeros((8, 128), jnp.float32), jnp.zeros((8, 128), jnp.float32)
                for g in range(BANDS):
                    at = pl.ds(PAD + 8 * (half * BANDS + g), 8)
                    top, bottom = q[depth + k, at], q[EDGE + k, at]
                    q[k, at] = roll(top, 1)
                    q[EDGE + depth + k, at] = roll(bottom, -1)
                    up = jnp.where(lanes % BANDS == g, roll(top, g + 1 - BANDS), up)
                    down = jnp.where(lanes % BANDS == g, roll(bottom, g), down)
                lat_out[step, 0, pl.ds(8 * (2 * k + half), 8)] = up
                lat_out[step, 1, pl.ds(8 * (2 * k + half), 8)] = down
        if now:
            send_lat_halos(step)

    def send_lat_halos(step):
        _, _, to_north, to_south = halo_copies(step)

        @pl.when(lat < 3)
        def _():
            to_north.start()

        @pl.when(lat > 0)
        def _():
            to_south.start()

    def send_halos(step):
        to_east, to_west, _, _ = halo_copies(step)
        to_east.start()
        to_west.start()
        send_lat_halos(step)

    def wait_halos(q, step):
        to_east, to_west, to_north, to_south = halo_copies(step)
        to_east.wait_recv()
        to_west.wait_recv()

        @pl.when(lat < 3)
        def _():
            to_south.wait_recv()

        @pl.when(lat > 0)
        def _():
            to_north.wait_recv()

        for r in range(depth):
            q[EDGE + r, pl.ds(PAD - EDGE, EDGE)] = lon_in[step, 0, pl.ds(EDGE * r, EDGE)]
            q[EDGE + r, pl.ds(PAD + columns, EDGE)] = lon_in[step, 1, pl.ds(EDGE * r, EDGE)]
        for k in range(EDGE):
            for half in range(2):
                below = lat_in[step, 0, pl.ds(8 * (2 * k + half), 8)]
                above = lat_in[step, 1, pl.ds(8 * (2 * k + half), 8)]
                for g in range(BANDS):
                    at = pl.ds(PAD + 8 * (half * BANDS + g), 8)
                    q[k, at] = jnp.where(lanes % BANDS == 0, roll(below, -g), q[k, at])
                    n = EDGE + depth + k
                    q[n, at] = jnp.where(lanes % BANDS == BANDS - 1, roll(above, BANDS - 1 - g), q[n, at])

    blank = jnp.zeros(lat_in.shape[2:], jnp.float32)
    for step in range(STEPS):

        @pl.when(lat == 0)
        def _():
            lat_in[step, 0] = blank

        @pl.when(lat == 3)
        def _():
            lat_in[step, 1] = blank


    across = pltpu.make_async_remote_copy(
        src_ref=send.at[1, :, pl.ds(0, used)], dst_ref=relay.at[:, pl.ds(0, used)],
        send_sem=core_send, recv_sem=core_recv, device_id=other, device_id_type=MESH,
    )

    def post(h, numbers):
        for i in numbers:
            src = send.at[0, i] if h == 0 else relay.at[i]
            pltpu.make_async_remote_copy(
                src_ref=src.at[pl.ds(0, used)], dst_ref=recv.at[h * PARTNERS + i, pl.ds(0, used)],
                send_sem=send_sem.at[h], recv_sem=recv_sem.at[h], device_id=partner(i), device_id_type=MESH,
            ).start()

    pl.semaphore_wait(barrier, LINES + 3)
    for i in range(1, LINES):
        pl.semaphore_signal(line_sem.at[0], inc=1, device_id=partner(i), device_id_type=MESH)
    across.start()
    post(0, range(1, LINES))
    for copy in loads[4:]:
        copy.start()
    recv[0] = send[0, 0]

    loads[3].wait()

    def turn_state(r):
        q0[r + EDGE, inner] = turned(raw_state, r)

    sweep(depth, 4, turn_state)

    start_halos(q0, 0)
    pl.semaphore_wait(line_sem.at[0], LINES - 1)
    for i in range(1, LINES):
        pl.semaphore_signal(line_sem.at[1], inc=1, device_id=partner(i), device_id_type=MESH)
    post(0, range(LINES, PLANES))
    pl.semaphore_wait(line_sem.at[1], LINES - 1)
    post(0, range(PLANES, PARTNERS))
    across.wait_recv()
    recv[PARTNERS] = relay[0]
    for numbers in (range(PLANES, PARTNERS), range(LINES, PLANES), range(1, LINES)):
        post(1, numbers)


    for copy in loads[4:]:
        copy.wait()

    def scale(n, carry):
        for b in range(rows // 32):
            at = (n, pl.ds(b * 32, 32))
            sea = raw_wet[at].astype(jnp.float32)
            raw_diff[at] = raw_diff[at] * sea
            raw_zonal[at] = raw_zonal[at] * sea * (1.0 / 12.0)
            raw_merid[at] = raw_merid[at] * sea * (1.0 / 12.0)
            scaled[at] = sea * (1.0 / STEPS)
        return carry

    lax.fori_loop(0, levels, scale, 0)
    for raw, ref in ((raw_diff, diff), (raw_zonal, zonal), (raw_merid, merid), (scaled, wet)):

        def turn(r):
            ref[r] = turned(raw, r)

        sweep(depth, 4, turn)

    def stencil(q, r, start, size):
        n, here_at = r + EDGE, pl.ds(PAD + start, size)
        here = q[n, here_at]
        east_cell, west_cell = q[n, pl.ds(PAD + start + 1, size)], q[n, pl.ds(PAD + start - 1, size)]
        far_east, far_west = q[n, pl.ds(PAD + start + 2, size)], q[n, pl.ds(PAD + start - 2, size)]
        north_cell, south_cell = q[n + 1, here_at], q[n - 1, here_at]
        far_north, far_south = q[n + 2, here_at], q[n - 2, here_at]
        at = (r, pl.ds(start, size))
        laplace = (east_cell + west_cell) + (north_cell + south_cell) - 4.0 * here
        along = 8.0 * (east_cell - west_cell) - (far_east - far_west)
        across = 8.0 * (north_cell - south_cell) - (far_north - far_south)
        return here + diff[at] * laplace - zonal[at] * along - merid[at] * across

    whole = [(32 * b, 32) for b in range(columns // 32)]
    middle = [(8, 32), (40, 32), (72, 32), (104, 16)]
    ends = [(0, 8), (columns - 8, 8)]

    wait_halos(q0, 0)

    def first_step(r):
        for start, size in whole:
            part[r, pl.ds(start, size)] = stencil(q0, r, start, size)

    sweep(depth, 2, first_step)

    place_row = lax.broadcasted_iota(jnp.int32, (rows, 128), 0)
    grid_row = (place_row % BANDS * depth + place_row // BANDS).astype(jnp.float32)
    slot_lane = lax.broadcasted_iota(jnp.int32, (1, 128), 1)
    flat = recv.reshape(recv.shape[0] * PIECE, columns)

    for h in range(2):
        a = recv.at[pl.ds(h * PARTNERS + 1, PARTNERS - 1), pl.ds(0, used)]
        pltpu.make_async_copy(a, a, recv_sem.at[h]).wait()

        def taken(n):
            return flat[pl.ds(h * PARTNERS * PIECE + n, PARTNERS, stride=PIECE), :]

        named_rows = taken(SLOTS * fields)
        rows_of = jnp.transpose(jnp.concatenate([named_rows] * SLOTS, axis=0))
        rows_of = jnp.where(slot_lane < PARTNERS, rows_of[0:1], rows_of[1:2])
        selector = jnp.where(grid_row == rows_of, 1.0, 0.0).astype(jnp.bfloat16)

        def assemble(n):
            data = jnp.concatenate([taken(s * fields + n) for s in range(SLOTS)], axis=0)
            high = data.astype(jnp.bfloat16)
            rest = (data - high.astype(jnp.float32)).astype(jnp.bfloat16)
            both = jnp.dot(selector, jnp.concatenate([high, rest], axis=1), preferred_element_type=jnp.float32)
            total = (both[:, :columns] + both[:, columns:]).reshape(depth, BANDS, columns)
            raw_force[n] = total if h == 0 else raw_force[n] + total

        sweep(fields, 8, assemble)

    def add_forcing(r):
        forcing = jnp.transpose(raw_force[:, r].reshape(fields * BANDS, columns)) * wet[r]
        force[r] = forcing
        q1[r + EDGE, inner] = part[r] + forcing

    sweep(depth, 4, add_forcing)

    def advance(q, r, start, size):
        return stencil(q, r, start, size) + force[r, pl.ds(start, size)]

    start_halos(q1, 1)

    def second_inside(r):
        for start, size in middle:
            q2[r + 2 * EDGE, pl.ds(PAD + start, size)] = advance(q1, r + EDGE, start, size)

    sweep(depth - 2 * EDGE, 2, second_inside)
    wait_halos(q1, 1)

    def second_ends(r):
        for start, size in ends:
            q2[r + 2 * EDGE, pl.ds(PAD + start, size)] = advance(q1, r + EDGE, start, size)

    sweep(depth - 2 * EDGE, 4, second_ends)
    for r in (0, 1, depth - 2, depth - 1):
        for start, size in whole:
            q2[r + EDGE, pl.ds(PAD + start, size)] = advance(q1, r, start, size)

    start_halos(q2, 2)

    def third_inside(r):
        for start, size in middle:
            part[r + EDGE, pl.ds(start, size)] = advance(q2, r + EDGE, start, size)

    sweep(depth - 2 * EDGE, 2, third_inside)
    wait_halos(q2, 2)

    def third_ends(r):
        for start, size in ends:
            part[r + EDGE, pl.ds(start, size)] = advance(q2, r + EDGE, start, size)

    sweep(depth - 2 * EDGE, 4, third_ends)
    for r in (0, 1, depth - 2, depth - 1):
        for start, size in whole:
            part[r, pl.ds(start, size)] = advance(q2, r, start, size)
    for step in range(STEPS):
        to_east, to_west, to_north, to_south = halo_copies(step)
        to_east.wait_send()
        to_west.wait_send()

        @pl.when(lat < 3)
        def _():
            to_north.wait_send()

        @pl.when(lat > 0)
        def _():
            to_south.wait_send()

    across.wait_send()
    for h in range(2):
        a = recv.at[pl.ds(h * PARTNERS + 1, PARTNERS - 1), pl.ds(0, used)]
        pltpu.make_async_copy(a, a, send_sem.at[h]).wait()


def turn_back(bands, out, result, out_sem):
    fields, _, depth, columns = out.shape
    flat = result.reshape((fields + 1) * BANDS * depth, columns)
    copies = []
    for group in range(depth // 8):
        for r in range(group * 8, group * 8 + 8):
            back = jnp.transpose(bands[r])
            for n in range(fields):
                flat[pl.ds(n * BANDS * depth + r, BANDS, stride=depth), :] = back[n * BANDS : (n + 1) * BANDS]
        rows = pl.ds(group * 8, 8)
        copy = pltpu.make_async_copy(
            result.at[pl.ds(0, fields), :, rows], out.at[:, :, rows], out_sem.at[group]
        )
        copy.start()
        copies.append(copy)
    for copy in copies:
        copy.wait()


def body(state, blocks, dest_tile, dest_row, kappa, lon_speed, lat_speed, sea_mask):
    tracers, levels, rows, columns = state.shape
    fields, depth = tracers * levels, rows // BANDS
    flat = (fields, rows, columns)
    f32, i32 = jnp.float32, jnp.int32
    anywhere = pl.BlockSpec(memory_space=pltpu.HBM)
    dma, vmem = pltpu.SemaphoreType.DMA, pltpu.VMEM
    tall = vmem((depth + 2 * EDGE, columns + 2 * PAD, 128), f32)
    turned = vmem((depth, columns, 128), f32)
    raw, coarse = vmem((fields + 1, rows, columns), f32), vmem((levels + 1, rows, columns), f32)
    bands = pl.pallas_call(
        kernel,
        out_shape=jax.ShapeDtypeStruct((depth, columns, 128), f32),
        in_specs=[anywhere] * 8,
        out_specs=pl.BlockSpec(memory_space=pltpu.VMEM),
        scratch_shapes=[
            vmem((1, 128), i32), vmem((1, 128), i32), vmem((128, fields, columns), f32),
            vmem((8, 128), i32), pltpu.SMEM((8, 128), i32), vmem((128, 128), f32),
            vmem((2, PARTNERS, PIECE, columns), f32), vmem((PARTNERS, PIECE, columns), f32),
            vmem((2 * PARTNERS + 1, PIECE, columns), f32),
            raw, coarse, coarse, coarse, vmem((levels, rows, columns), i32),
            vmem((fields, depth, BANDS, columns), f32), coarse,
            tall, tall, tall, turned, turned, turned, turned, turned,
            vmem((STEPS, 2, EDGE * depth, 128), f32), vmem((STEPS, 2, EDGE * depth, 128), f32),
            vmem((STEPS, 2, 16 * EDGE, 128), f32), vmem((STEPS, 2, 16 * EDGE, 128), f32),
            dma((8,)), dma, pltpu.SemaphoreType.REGULAR((2,)), dma, dma, dma((2,)), dma((2,)), dma((STEPS, 4)), dma((STEPS, 4)),
        ],
        compiler_params=pltpu.CompilerParams(
            collective_id=0, has_side_effects=True, vmem_limit_bytes=VL << 20
        ),
    )(*[
        pltpu.with_memory_space_constraint(x, pltpu.HBM)
        for x in (
            state.reshape(flat), blocks.reshape(128, fields, columns), dest_tile.reshape(1, 128),
            dest_row.reshape(1, 128), kappa, lon_speed, lat_speed, sea_mask,
        )
    ])
    result = pl.pallas_call(
        turn_back,
        out_shape=jax.ShapeDtypeStruct((fields, BANDS, depth, columns), f32),
        in_specs=[pl.BlockSpec(memory_space=pltpu.VMEM)],
        out_specs=anywhere,
        scratch_shapes=[vmem((fields + 1, BANDS, depth, columns), f32), dma((depth // 8,))],
        compiler_params=pltpu.CompilerParams(vmem_limit_bytes=16 << 20),
    )(bands)
    return result.reshape(state.shape)


def solution(mesh):
    placed = (
        P(None, None, "lat", "lon"),
        P(("lon", "lat"), None, None, None),
        P(("lon", "lat"), None),
        P(("lon", "lat")),
        P(None, "lat", "lon"),
        P(None, "lat", "lon"),
        P(None, "lat", "lon"),
        P(None, "lat", "lon"),
    )
    return jax.shard_map(
        body, mesh=mesh, in_specs=placed, out_specs=P(None, None, "lat", "lon"), check_vma=False
    )
```

```python
import jax
import jax.numpy as jnp
from jax import lax
from jax.experimental import pallas as pl
from jax.experimental.pallas import tpu as pltpu
from jax.sharding import PartitionSpec as P

MESH = pl.DeviceIdType.MESH
STEPS = 3
BANDS = 8
PARTNERS = 64
SLOTS = 2
PIECE = 40
VL = 44
PAD = 8
EDGE = 2
OFFSETS = sorted(
    ((z, x, y) for z in range(4) for x in range(4) for y in range(4)),
    key=lambda o: (sum(d > 0 for d in o), -sum(d == 2 for d in o), (16 * o[0] + 4 * o[1] + o[2]) * 27 % 64),
)
LINES, PLANES = 10, 37


def roll(x, amount):
    amount = amount % 128
    return x if amount == 0 else pltpu.roll(x, amount, 1)


def kernel(
    state, blocks, tile_at, row_at, kappa, lon_speed, lat_speed, mask, part,
    tile_ref, row_ref, held, table, table_s, plan, send, relay, recv,
    raw_state, raw_diff, raw_zonal, raw_merid, raw_wet, raw_force, scaled,
    q0, q1, q2, force, diff, zonal, merid, wet, lon_out, lon_in, lat_out, lat_in,
    load_sem, table_sem, line_sem, core_send, core_recv, send_sem, recv_sem, halo_send, halo_recv,
):
    levels, rows, columns = kappa.shape
    fields = state.shape[0]
    depth = rows // BANDS
    used = (SLOTS * fields, SLOTS * fields + 1)
    lon, lat = lax.axis_index("lon"), lax.axis_index("lat")
    core = lat % 2
    z, x, y = lon // 8, (lat // 2) * 2 + (lon // 4) % 2, lon % 4
    other = (lon, lat + 1 - 2 * core)

    def place(i):
        dz, dx, dy = OFFSETS[i]
        return (z + dz) % 4, (x + dx) % 4, (y + dy) % 4

    def partner(i):
        z, x, y = place(i)
        return (z * 8 + (x % 2) * 4 + y, (x // 2) * 2 + core)

    moves = (
        (tile_at, tile_ref), (row_at, row_ref), (blocks, held), (state, raw_state.at[pl.ds(0, fields)]),
        (kappa, raw_diff.at[pl.ds(0, levels)]), (lon_speed, raw_zonal.at[pl.ds(0, levels)]),
        (lat_speed, raw_merid.at[pl.ds(0, levels)]), (mask, raw_wet),
    )
    loads = [pltpu.make_async_copy(src, dst, load_sem.at[k]) for k, (src, dst) in enumerate(moves)]
    for copy in loads[:4]:
        copy.start()
    east, west = ((lon + 1) % 32, lat), ((lon + 31) % 32, lat)

    barrier = pltpu.get_barrier_semaphore()
    for device in [partner(i) for i in range(1, LINES)] + [other, (lon, 3 - lat), east, west]:
        pl.semaphore_signal(barrier, inc=1, device_id=device, device_id_type=MESH)
    loads[0].wait()
    loads[1].wait()

    tile_of = lax.broadcasted_iota(jnp.int32, (128, 128), 0)
    number = lax.broadcasted_iota(jnp.int32, (128, 128), 1)
    named = tile_ref[...] == tile_of
    first = jnp.min(jnp.where(named, number, 128), axis=1, keepdims=True)
    last = jnp.max(jnp.where(named, number, -1), axis=1, keepdims=True)
    row_f = row_ref[...].astype(jnp.float32)
    first_row = jnp.sum(jnp.where(number == first, row_f, 0.0), axis=1, keepdims=True)
    last_row = jnp.sum(jnp.where(number == last, row_f, 0.0), axis=1, keepdims=True)
    first_row = jnp.where(last >= 0, first_row, -1.0)
    last_row = jnp.where(last > first, last_row, -1.0)
    plan[...] = jnp.where(number % SLOTS == 0, first_row, last_row)
    slots = jnp.where(number == 0, jnp.minimum(first, 127), jnp.maximum(last, 0))
    table[...] = jnp.transpose(slots)[:8]
    to_scalars = pltpu.make_async_copy(table, table_s, table_sem)
    to_scalars.start()
    loads[2].wait()
    to_scalars.wait()

    def tile(h, i):
        tz, tx, ty = place(i)
        return tz * 32 + (tx % 2) * 16 + ty * 4 + (tx // 2) * 2 + (core if h == 0 else 1 - core)

    def pack(h, numbers):
        for i in numbers:
            for s in range(SLOTS):
                send[h, i, pl.ds(s * fields, fields)] = held[table_s[s, tile(h, i)]]
            if h == 1:
                send[h, i, pl.ds(SLOTS * fields, 1)] = plan[pl.ds(tile(h, i), 1), :]

    pack(1, range(PARTNERS))
    pack(0, range(PARTNERS))

    def turned(ref, r):
        flat = ref.reshape(ref.shape[0] * rows, columns)
        count = ref.shape[0] - 1
        taken = [flat[pl.ds(n * rows + r, BANDS, stride=depth), :] for n in range(count)]
        return jnp.transpose(jnp.concatenate(taken * (fields // count), axis=0))

    def sweep(count, unroll, step):
        def some(i, carry):
            for k in range(unroll):
                step(i * unroll + k)
            return carry

        lax.fori_loop(0, count // unroll, some, 0)

    inner = pl.ds(PAD, columns)

    lanes = lax.broadcasted_iota(jnp.int32, (8, 128), 1)

    def halo_copy(src, dst, step, k, device):
        return pltpu.make_async_remote_copy(
            src_ref=src, dst_ref=dst, send_sem=halo_send.at[step, k], recv_sem=halo_recv.at[step, k],
            device_id=device, device_id_type=MESH,
        )

    def lon_copies(step, half):
        return [
            halo_copy(lon_out.at[step, d, half], lon_in.at[step, d, half], step, 2 * half + d, device)
            for d, device in enumerate((east, west))
        ]

    def lat_copies(step):
        return [
            halo_copy(lat_out.at[step, d], lat_in.at[step, d], step, 4 + d, (lon, there))
            for d, there in enumerate((jnp.minimum(lat + 1, 3), jnp.maximum(lat - 1, 0)))
        ]

    half_depth = depth // 2

    def start_lon(q, step, half):
        for k in range(half_depth):
            n, at = EDGE + half * half_depth + k, pl.ds(EDGE * k, EDGE)
            lon_out[step, 0, half, at] = q[n, pl.ds(PAD + columns - EDGE, EDGE)]
            lon_out[step, 1, half, at] = q[n, pl.ds(PAD, EDGE)]
        for copy in lon_copies(step, half):
            copy.start()

    def start_lat(q, step):
        for k in range(EDGE):
            for half in range(2):
                up, down = jnp.zeros((8, 128), jnp.float32), jnp.zeros((8, 128), jnp.float32)
                for g in range(BANDS):
                    at = pl.ds(PAD + 8 * (half * BANDS + g), 8)
                    top, bottom = q[depth + k, at], q[EDGE + k, at]
                    q[k, at] = roll(top, 1)
                    q[EDGE + depth + k, at] = roll(bottom, -1)
                    up = jnp.where(lanes % BANDS == g, roll(top, g + 1 - BANDS), up)
                    down = jnp.where(lanes % BANDS == g, roll(bottom, g), down)
                lat_out[step, 0, pl.ds(8 * (2 * k + half), 8)] = up
                lat_out[step, 1, pl.ds(8 * (2 * k + half), 8)] = down
        to_north, to_south = lat_copies(step)

        @pl.when(lat < 3)
        def _():
            to_north.start()

        @pl.when(lat > 0)
        def _():
            to_south.start()

    def wait_lon(q, step, half):
        for copy in lon_copies(step, half):
            copy.wait_recv()
        for k in range(half_depth):
            n, at = EDGE + half * half_depth + k, pl.ds(EDGE * k, EDGE)
            q[n, pl.ds(PAD - EDGE, EDGE)] = lon_in[step, 0, half, at]
            q[n, pl.ds(PAD + columns, EDGE)] = lon_in[step, 1, half, at]

    def wait_lat(q, step):
        to_north, to_south = lat_copies(step)

        @pl.when(lat < 3)
        def _():
            to_south.wait_recv()

        @pl.when(lat > 0)
        def _():
            to_north.wait_recv()

        for k in range(EDGE):
            for half in range(2):
                below = lat_in[step, 0, pl.ds(8 * (2 * k + half), 8)]
                above = lat_in[step, 1, pl.ds(8 * (2 * k + half), 8)]
                for g in range(BANDS):
                    at = pl.ds(PAD + 8 * (half * BANDS + g), 8)
                    q[k, at] = jnp.where(lanes % BANDS == 0, roll(below, -g), q[k, at])
                    n = EDGE + depth + k
                    q[n, at] = jnp.where(lanes % BANDS == BANDS - 1, roll(above, BANDS - 1 - g), q[n, at])

    blank = jnp.zeros(lat_in.shape[2:], jnp.float32)
    for step in range(STEPS):

        @pl.when(lat == 0)
        def _():
            lat_in[step, 0] = blank

        @pl.when(lat == 3)
        def _():
            lat_in[step, 1] = blank


    across = pltpu.make_async_remote_copy(
        src_ref=send.at[1, :, pl.ds(0, used[1])], dst_ref=relay.at[:, pl.ds(0, used[1])],
        send_sem=core_send, recv_sem=core_recv, device_id=other, device_id_type=MESH,
    )

    slot_lane = lax.broadcasted_iota(jnp.int32, (1, 128), 1)

    def post(h, numbers):
        for i in numbers:
            src = send.at[0, i] if h == 0 else relay.at[i]
            pltpu.make_async_remote_copy(
                src_ref=src.at[pl.ds(0, used[h])], dst_ref=recv.at[h * PARTNERS + i, pl.ds(0, used[h])],
                send_sem=send_sem.at[h], recv_sem=recv_sem.at[h], device_id=partner(i), device_id_type=MESH,
            ).start()

    pl.semaphore_wait(barrier, LINES + 3)
    for i in range(1, LINES):
        pl.semaphore_signal(line_sem.at[0], inc=1, device_id=partner(i), device_id_type=MESH)
    across.start()
    post(0, range(1, LINES))
    for copy in loads[4:]:
        copy.start()
    recv[0] = send[0, 0]

    loads[3].wait()

    def turn_state(r):
        q0[r + EDGE, inner] = turned(raw_state, r)

    sweep(depth, 4, turn_state)

    for half in range(2):
        start_lon(q0, 0, half)
    start_lat(q0, 0)
    pl.semaphore_wait(line_sem.at[0], LINES - 1)
    for i in range(1, LINES):
        pl.semaphore_signal(line_sem.at[1], inc=1, device_id=partner(i), device_id_type=MESH)
    post(0, range(LINES, PLANES))
    pl.semaphore_wait(line_sem.at[1], LINES - 1)
    post(0, range(PLANES, PARTNERS))
    across.wait_recv()
    for i in range(PARTNERS):
        at = (i, pl.ds(SLOTS * fields, 1))
        relay[at] = jnp.where(slot_lane < SLOTS, relay[at], plan[pl.ds(tile(0, i), 1), :])
    recv[PARTNERS] = relay[0]
    for numbers in (range(PLANES, PARTNERS), range(LINES, PLANES), range(1, LINES)):
        post(1, numbers)


    for copy in loads[4:]:
        copy.wait()

    def scale(n, carry):
        for b in range(rows // 32):
            at = (n, pl.ds(b * 32, 32))
            sea = raw_wet[at].astype(jnp.float32)
            raw_diff[at] = raw_diff[at] * sea
            raw_zonal[at] = raw_zonal[at] * sea * (1.0 / 12.0)
            raw_merid[at] = raw_merid[at] * sea * (1.0 / 12.0)
            scaled[at] = sea * (1.0 / STEPS)
        return carry

    lax.fori_loop(0, levels, scale, 0)
    for raw, ref in ((raw_diff, diff), (raw_zonal, zonal), (raw_merid, merid), (scaled, wet)):

        def turn(r):
            ref[r] = turned(raw, r)

        sweep(depth, 4, turn)

    def stencil(q, r, start, size):
        n, here_at = r + EDGE, pl.ds(PAD + start, size)
        here = q[n, here_at]
        east_cell, west_cell = q[n, pl.ds(PAD + start + 1, size)], q[n, pl.ds(PAD + start - 1, size)]
        far_east, far_west = q[n, pl.ds(PAD + start + 2, size)], q[n, pl.ds(PAD + start - 2, size)]
        north_cell, south_cell = q[n + 1, here_at], q[n - 1, here_at]
        far_north, far_south = q[n + 2, here_at], q[n - 2, here_at]
        at = (r, pl.ds(start, size))
        laplace = (east_cell + west_cell) + (north_cell + south_cell) - 4.0 * here
        along = 8.0 * (east_cell - west_cell) - (far_east - far_west)
        across = 8.0 * (north_cell - south_cell) - (far_north - far_south)
        return here + diff[at] * laplace - zonal[at] * along - merid[at] * across

    whole = [(32 * b, 32) for b in range(columns // 32)]
    middle = [(8, 32), (40, 32), (72, 32), (104, 16)]
    ends = [(0, 8), (columns - 8, 8)]

    wait_lat(q0, 0)
    for half in range(2):
        wait_lon(q0, 0, half)

    def first_step(r):
        for start, size in whole:
            part[r, pl.ds(start, size)] = stencil(q0, r, start, size)

    sweep(depth, 2, first_step)

    for h in range(2):
        a = recv.at[pl.ds(h * PARTNERS + 1, PARTNERS - 1), pl.ds(0, used[h])]
        pltpu.make_async_copy(a, a, recv_sem.at[h]).wait()
    place_row = lax.broadcasted_iota(jnp.int32, (rows, 128), 0)
    grid_row = (place_row % BANDS * depth + place_row // BANDS).astype(jnp.float32)
    flat = recv.reshape(recv.shape[0] * PIECE, columns)

    def taken(h, n):
        return flat[pl.ds(h * PARTNERS * PIECE + n, PARTNERS, stride=PIECE), :]

    rows_of = jnp.transpose(jnp.concatenate([taken(1, SLOTS * fields)] * SLOTS, axis=0))
    selector = []
    for h in range(2):
        own = SLOTS * (1 - h)
        named_rows = jnp.where(slot_lane < PARTNERS, rows_of[own : own + 1], rows_of[own + 1 : own + 2])
        selector.append(jnp.where(grid_row == named_rows, 1.0, 0.0).astype(jnp.bfloat16))
    selector = jnp.concatenate(selector, axis=1)

    def assemble(n):
        data = jnp.concatenate([taken(h, s * fields + n) for h in range(2) for s in range(SLOTS)], axis=0)
        high = data.astype(jnp.bfloat16)
        rest = (data - high.astype(jnp.float32)).astype(jnp.bfloat16)
        both = jnp.dot(selector, jnp.concatenate([high, rest], axis=1), preferred_element_type=jnp.float32)
        raw_force[n] = (both[:, :columns] + both[:, columns:]).reshape(depth, BANDS, columns)

    sweep(fields, 8, assemble)

    def add_forcing(r):
        forcing = jnp.transpose(raw_force[:, r].reshape(fields * BANDS, columns)) * wet[r]
        force[r] = forcing
        q1[r + EDGE, inner] = part[r] + forcing

    def sweep_from(start, count, unroll, step):
        sweep(count, unroll, lambda r: step(r + start))

    for half in range(2):
        sweep_from(half * half_depth, half_depth, 4, add_forcing)
        start_lon(q1, 1, half)
    start_lat(q1, 1)

    def advance(q, r, start, size):
        return stencil(q, r, start, size) + force[r, pl.ds(start, size)]

    def second(spans):
        def step(r):
            for start, size in spans:
                q2[r + EDGE, pl.ds(PAD + start, size)] = advance(q1, r, start, size)

        return step

    def third(spans):
        def step(r):
            for start, size in spans:
                part[r, pl.ds(start, size)] = advance(q2, r, start, size)

        return step

    def outside(step, half):
        sweep_from(EDGE + half * (half_depth - EDGE), half_depth - EDGE, 2, step(ends))
        for r in (0, 1) if half == 0 else (depth - 2, depth - 1):
            step(whole)(r)

    sweep_from(EDGE, depth - 2 * EDGE, 2, second(middle))
    wait_lat(q1, 1)
    for half in range(2):
        wait_lon(q1, 1, half)
        outside(second, half)
        start_lon(q2, 2, half)
    start_lat(q2, 2)
    sweep_from(EDGE, depth - 2 * EDGE, 2, third(middle))
    wait_lat(q2, 2)
    for half in range(2):
        wait_lon(q2, 2, half)
        outside(third, half)

    for step in range(STEPS):
        for half in range(2):
            for copy in lon_copies(step, half):
                copy.wait_send()
        to_north, to_south = lat_copies(step)

        @pl.when(lat < 3)
        def _():
            to_north.wait_send()

        @pl.when(lat > 0)
        def _():
            to_south.wait_send()

    across.wait_send()
    for h in range(2):
        a = recv.at[pl.ds(h * PARTNERS + 1, PARTNERS - 1), pl.ds(0, used[h])]
        pltpu.make_async_copy(a, a, send_sem.at[h]).wait()


def turn_back(bands, out, result, out_sem):
    fields, _, depth, columns = out.shape
    flat = result.reshape((fields + 1) * BANDS * depth, columns)
    copies = []
    for group in range(depth // 8):
        for r in range(group * 8, group * 8 + 8):
            back = jnp.transpose(bands[r])
            for n in range(fields):
                flat[pl.ds(n * BANDS * depth + r, BANDS, stride=depth), :] = back[n * BANDS : (n + 1) * BANDS]
        rows = pl.ds(group * 8, 8)
        copy = pltpu.make_async_copy(
            result.at[pl.ds(0, fields), :, rows], out.at[:, :, rows], out_sem.at[group]
        )
        copy.start()
        copies.append(copy)
    for copy in copies:
        copy.wait()


def body(state, blocks, dest_tile, dest_row, kappa, lon_speed, lat_speed, sea_mask):
    tracers, levels, rows, columns = state.shape
    fields, depth = tracers * levels, rows // BANDS
    flat = (fields, rows, columns)
    f32, i32 = jnp.float32, jnp.int32
    anywhere = pl.BlockSpec(memory_space=pltpu.HBM)
    dma, vmem = pltpu.SemaphoreType.DMA, pltpu.VMEM
    tall = vmem((depth + 2 * EDGE, columns + 2 * PAD, 128), f32)
    turned = vmem((depth, columns, 128), f32)
    raw, coarse = vmem((fields + 1, rows, columns), f32), vmem((levels + 1, rows, columns), f32)
    bands = pl.pallas_call(
        kernel,
        out_shape=jax.ShapeDtypeStruct((depth, columns, 128), f32),
        in_specs=[anywhere] * 8,
        out_specs=pl.BlockSpec(memory_space=pltpu.VMEM),
        scratch_shapes=[
            vmem((1, 128), i32), vmem((1, 128), i32), vmem((128, fields, columns), f32),
            vmem((8, 128), i32), pltpu.SMEM((8, 128), i32), vmem((128, 128), f32),
            vmem((2, PARTNERS, PIECE, columns), f32), vmem((PARTNERS, PIECE, columns), f32),
            vmem((2 * PARTNERS + 1, PIECE, columns), f32),
            raw, coarse, coarse, coarse, vmem((levels, rows, columns), i32),
            vmem((fields, depth, BANDS, columns), f32), coarse,
            tall, tall, tall, turned, turned, turned, turned, turned,
            vmem((STEPS, 2, 2, EDGE * depth // 2, 128), f32), vmem((STEPS, 2, 2, EDGE * depth // 2, 128), f32),
            vmem((STEPS, 2, 16 * EDGE, 128), f32), vmem((STEPS, 2, 16 * EDGE, 128), f32),
            dma((8,)), dma, pltpu.SemaphoreType.REGULAR((2,)), dma, dma, dma((2,)), dma((2,)), dma((STEPS, 6)), dma((STEPS, 6)),
        ],
        compiler_params=pltpu.CompilerParams(
            collective_id=0, has_side_effects=True, vmem_limit_bytes=VL << 20
        ),
    )(*[
        pltpu.with_memory_space_constraint(x, pltpu.HBM)
        for x in (
            state.reshape(flat), blocks.reshape(128, fields, columns), dest_tile.reshape(1, 128),
            dest_row.reshape(1, 128), kappa, lon_speed, lat_speed, sea_mask,
        )
    ])
    result = pl.pallas_call(
        turn_back,
        out_shape=jax.ShapeDtypeStruct((fields, BANDS, depth, columns), f32),
        in_specs=[pl.BlockSpec(memory_space=pltpu.VMEM)],
        out_specs=anywhere,
        scratch_shapes=[vmem((fields + 1, BANDS, depth, columns), f32), dma((depth // 8,))],
        compiler_params=pltpu.CompilerParams(vmem_limit_bytes=16 << 20),
    )(bands)
    return result.reshape(state.shape)


def solution(mesh):
    placed = (
        P(None, None, "lat", "lon"),
        P(("lon", "lat"), None, None, None),
        P(("lon", "lat"), None),
        P(("lon", "lat")),
        P(None, "lat", "lon"),
        P(None, "lat", "lon"),
        P(None, "lat", "lon"),
        P(None, "lat", "lon"),
    )
    return jax.shard_map(
        body, mesh=mesh, in_specs=placed, out_specs=P(None, None, "lat", "lon"), check_vma=False
    )
```

```python
import jax
import jax.numpy as jnp
from jax import lax
from jax.experimental import pallas as pl
from jax.experimental.pallas import tpu as pltpu
from jax.sharding import PartitionSpec as P

MESH = pl.DeviceIdType.MESH
STEPS = 3
BANDS = 8
PARTNERS = 64
SLOTS = 2
PIECE = 40
VL = 44
PAD = 8
EDGE = 2
PARTS = 4
OFFSETS = sorted(
    ((z, x, y) for z in range(4) for x in range(4) for y in range(4)),
    key=lambda o: (sum(d > 0 for d in o), -sum(d == 2 for d in o), (16 * o[0] + 4 * o[1] + o[2]) * 27 % 64),
)
LINES, PLANES = 10, 37


def roll(x, amount):
    amount = amount % 128
    return x if amount == 0 else pltpu.roll(x, amount, 1)


def kernel(
    state, blocks, tile_at, row_at, kappa, lon_speed, lat_speed, mask, part,
    tile_ref, row_ref, held, table, table_s, plan, send, relay, recv,
    raw_state, raw_diff, raw_zonal, raw_merid, raw_wet, raw_force, scaled,
    q0, q1, q2, force, diff, zonal, merid, wet, lon_out, lon_in, lat_out, lat_in,
    load_sem, table_sem, line_sem, core_send, core_recv, send_sem, recv_sem, halo_send, halo_recv,
):
    levels, rows, columns = kappa.shape
    fields = state.shape[0]
    depth = rows // BANDS
    used = (SLOTS * fields, SLOTS * fields + 1)
    lon, lat = lax.axis_index("lon"), lax.axis_index("lat")
    core = lat % 2
    z, x, y = lon // 8, (lat // 2) * 2 + (lon // 4) % 2, lon % 4
    other = (lon, lat + 1 - 2 * core)

    def place(i):
        dz, dx, dy = OFFSETS[i]
        return (z + dz) % 4, (x + dx) % 4, (y + dy) % 4

    def partner(i):
        z, x, y = place(i)
        return (z * 8 + (x % 2) * 4 + y, (x // 2) * 2 + core)

    moves = (
        (tile_at, tile_ref), (row_at, row_ref), (blocks, held), (state, raw_state.at[pl.ds(0, fields)]),
        (kappa, raw_diff.at[pl.ds(0, levels)]), (lon_speed, raw_zonal.at[pl.ds(0, levels)]),
        (lat_speed, raw_merid.at[pl.ds(0, levels)]), (mask, raw_wet),
    )
    loads = [pltpu.make_async_copy(src, dst, load_sem.at[k]) for k, (src, dst) in enumerate(moves)]
    for copy in loads[:4]:
        copy.start()
    east, west = ((lon + 1) % 32, lat), ((lon + 31) % 32, lat)

    barrier = pltpu.get_barrier_semaphore()
    for device in [partner(i) for i in range(1, LINES)] + [other, (lon, 3 - lat), east, west]:
        pl.semaphore_signal(barrier, inc=1, device_id=device, device_id_type=MESH)
    loads[0].wait()
    loads[1].wait()

    tile_of = lax.broadcasted_iota(jnp.int32, (128, 128), 0)
    number = lax.broadcasted_iota(jnp.int32, (128, 128), 1)
    named = tile_ref[...] == tile_of
    first = jnp.min(jnp.where(named, number, 128), axis=1, keepdims=True)
    last = jnp.max(jnp.where(named, number, -1), axis=1, keepdims=True)
    row_f = row_ref[...].astype(jnp.float32)
    first_row = jnp.sum(jnp.where(number == first, row_f, 0.0), axis=1, keepdims=True)
    last_row = jnp.sum(jnp.where(number == last, row_f, 0.0), axis=1, keepdims=True)
    first_row = jnp.where(last >= 0, first_row, -1.0)
    last_row = jnp.where(last > first, last_row, -1.0)
    plan[...] = jnp.where(number % SLOTS == 0, first_row, last_row)
    slots = jnp.where(number == 0, jnp.minimum(first, 127), jnp.maximum(last, 0))
    table[...] = jnp.transpose(slots)[:8]
    to_scalars = pltpu.make_async_copy(table, table_s, table_sem)
    to_scalars.start()
    loads[2].wait()
    to_scalars.wait()

    def tile(h, i):
        tz, tx, ty = place(i)
        return tz * 32 + (tx % 2) * 16 + ty * 4 + (tx // 2) * 2 + (core if h == 0 else 1 - core)

    def pack(h, numbers):
        for i in numbers:
            for s in range(SLOTS):
                send[h, i, pl.ds(s * fields, fields)] = held[table_s[s, tile(h, i)]]
            if h == 1:
                send[h, i, pl.ds(SLOTS * fields, 1)] = plan[pl.ds(tile(h, i), 1), :]

    pack(1, range(PARTNERS))
    pack(0, range(PARTNERS))

    def turned(ref, r):
        flat = ref.reshape(ref.shape[0] * rows, columns)
        count = ref.shape[0] - 1
        taken = [flat[pl.ds(n * rows + r, BANDS, stride=depth), :] for n in range(count)]
        return jnp.transpose(jnp.concatenate(taken * (fields // count), axis=0))

    def sweep(count, unroll, step):
        def some(i, carry):
            for k in range(unroll):
                step(i * unroll + k)
            return carry

        lax.fori_loop(0, count // unroll, some, 0)

    inner = pl.ds(PAD, columns)

    lanes = lax.broadcasted_iota(jnp.int32, (8, 128), 1)

    def halo_copy(src, dst, step, k, device):
        return pltpu.make_async_remote_copy(
            src_ref=src, dst_ref=dst, send_sem=halo_send.at[step, k], recv_sem=halo_recv.at[step, k],
            device_id=device, device_id_type=MESH,
        )

    def lon_copies(step, p):
        return [
            halo_copy(lon_out.at[step, d, p], lon_in.at[step, d, p], step, 2 * p + d, device)
            for d, device in enumerate((east, west))
        ]

    def lat_copies(step):
        return [
            halo_copy(lat_out.at[step, d], lat_in.at[step, d], step, 2 * PARTS + d, (lon, there))
            for d, there in enumerate((jnp.minimum(lat + 1, 3), jnp.maximum(lat - 1, 0)))
        ]

    some_rows = depth // PARTS

    def start_lon(q, step, p):
        for k in range(some_rows):
            n, at = EDGE + p * some_rows + k, pl.ds(EDGE * k, EDGE)
            lon_out[step, 0, p, at] = q[n, pl.ds(PAD + columns - EDGE, EDGE)]
            lon_out[step, 1, p, at] = q[n, pl.ds(PAD, EDGE)]
        for copy in lon_copies(step, p):
            copy.start()

    def start_lat(q, step):
        for k in range(EDGE):
            for half in range(2):
                up, down = jnp.zeros((8, 128), jnp.float32), jnp.zeros((8, 128), jnp.float32)
                for g in range(BANDS):
                    at = pl.ds(PAD + 8 * (half * BANDS + g), 8)
                    top, bottom = q[depth + k, at], q[EDGE + k, at]
                    q[k, at] = roll(top, 1)
                    q[EDGE + depth + k, at] = roll(bottom, -1)
                    up = jnp.where(lanes % BANDS == g, roll(top, g + 1 - BANDS), up)
                    down = jnp.where(lanes % BANDS == g, roll(bottom, g), down)
                lat_out[step, 0, pl.ds(8 * (2 * k + half), 8)] = up
                lat_out[step, 1, pl.ds(8 * (2 * k + half), 8)] = down
        to_north, to_south = lat_copies(step)

        @pl.when(lat < 3)
        def _():
            to_north.start()

        @pl.when(lat > 0)
        def _():
            to_south.start()

    def wait_lon(q, step, p):
        for copy in lon_copies(step, p):
            copy.wait_recv()
        for k in range(some_rows):
            n, at = EDGE + p * some_rows + k, pl.ds(EDGE * k, EDGE)
            q[n, pl.ds(PAD - EDGE, EDGE)] = lon_in[step, 0, p, at]
            q[n, pl.ds(PAD + columns, EDGE)] = lon_in[step, 1, p, at]

    def wait_lat(q, step):
        to_north, to_south = lat_copies(step)

        @pl.when(lat < 3)
        def _():
            to_south.wait_recv()

        @pl.when(lat > 0)
        def _():
            to_north.wait_recv()

        for k in range(EDGE):
            for half in range(2):
                below = lat_in[step, 0, pl.ds(8 * (2 * k + half), 8)]
                above = lat_in[step, 1, pl.ds(8 * (2 * k + half), 8)]
                for g in range(BANDS):
                    at = pl.ds(PAD + 8 * (half * BANDS + g), 8)
                    q[k, at] = jnp.where(lanes % BANDS == 0, roll(below, -g), q[k, at])
                    n = EDGE + depth + k
                    q[n, at] = jnp.where(lanes % BANDS == BANDS - 1, roll(above, BANDS - 1 - g), q[n, at])

    blank = jnp.zeros(lat_in.shape[2:], jnp.float32)
    for step in range(STEPS):

        @pl.when(lat == 0)
        def _():
            lat_in[step, 0] = blank

        @pl.when(lat == 3)
        def _():
            lat_in[step, 1] = blank


    across = pltpu.make_async_remote_copy(
        src_ref=send.at[1, :, pl.ds(0, used[1])], dst_ref=relay.at[:, pl.ds(0, used[1])],
        send_sem=core_send, recv_sem=core_recv, device_id=other, device_id_type=MESH,
    )

    slot_lane = lax.broadcasted_iota(jnp.int32, (1, 128), 1)

    def post(h, numbers):
        for i in numbers:
            src = send.at[0, i] if h == 0 else relay.at[i]
            pltpu.make_async_remote_copy(
                src_ref=src.at[pl.ds(0, used[h])], dst_ref=recv.at[h * PARTNERS + i, pl.ds(0, used[h])],
                send_sem=send_sem.at[h], recv_sem=recv_sem.at[h], device_id=partner(i), device_id_type=MESH,
            ).start()

    pl.semaphore_wait(barrier, LINES + 3)
    for i in range(1, LINES):
        pl.semaphore_signal(line_sem.at[0], inc=1, device_id=partner(i), device_id_type=MESH)
    across.start()
    post(0, range(1, LINES))
    for copy in loads[4:]:
        copy.start()
    recv[0] = send[0, 0]

    loads[3].wait()

    def turn_state(r):
        q0[r + EDGE, inner] = turned(raw_state, r)

    sweep(depth, 4, turn_state)

    for p in range(PARTS):
        start_lon(q0, 0, p)
    start_lat(q0, 0)
    pl.semaphore_wait(line_sem.at[0], LINES - 1)
    for i in range(1, LINES):
        pl.semaphore_signal(line_sem.at[1], inc=1, device_id=partner(i), device_id_type=MESH)
    post(0, range(LINES, PLANES))
    pl.semaphore_wait(line_sem.at[1], LINES - 1)
    post(0, range(PLANES, PARTNERS))
    across.wait_recv()
    for i in range(PARTNERS):
        at = (i, pl.ds(SLOTS * fields, 1))
        relay[at] = jnp.where(slot_lane < SLOTS, relay[at], plan[pl.ds(tile(0, i), 1), :])
    recv[PARTNERS] = relay[0]
    for numbers in (range(PLANES, PARTNERS), range(LINES, PLANES), range(1, LINES)):
        post(1, numbers)


    for copy in loads[4:]:
        copy.wait()

    def scale(n, carry):
        for b in range(rows // 32):
            at = (n, pl.ds(b * 32, 32))
            sea = raw_wet[at].astype(jnp.float32)
            raw_diff[at] = raw_diff[at] * sea
            raw_zonal[at] = raw_zonal[at] * sea * (1.0 / 12.0)
            raw_merid[at] = raw_merid[at] * sea * (1.0 / 12.0)
            scaled[at] = sea * (1.0 / STEPS)
        return carry

    lax.fori_loop(0, levels, scale, 0)
    for raw, ref in ((raw_diff, diff), (raw_zonal, zonal), (raw_merid, merid), (scaled, wet)):

        def turn(r):
            ref[r] = turned(raw, r)

        sweep(depth, 4, turn)

    def stencil(q, r, start, size):
        n, here_at = r + EDGE, pl.ds(PAD + start, size)
        here = q[n, here_at]
        east_cell, west_cell = q[n, pl.ds(PAD + start + 1, size)], q[n, pl.ds(PAD + start - 1, size)]
        far_east, far_west = q[n, pl.ds(PAD + start + 2, size)], q[n, pl.ds(PAD + start - 2, size)]
        north_cell, south_cell = q[n + 1, here_at], q[n - 1, here_at]
        far_north, far_south = q[n + 2, here_at], q[n - 2, here_at]
        at = (r, pl.ds(start, size))
        laplace = (east_cell + west_cell) + (north_cell + south_cell) - 4.0 * here
        along = 8.0 * (east_cell - west_cell) - (far_east - far_west)
        across = 8.0 * (north_cell - south_cell) - (far_north - far_south)
        return here + diff[at] * laplace - zonal[at] * along - merid[at] * across

    whole = [(32 * b, 32) for b in range(columns // 32)]
    middle = [(8, 32), (40, 32), (72, 32), (104, 16)]
    ends = [(0, 8), (columns - 8, 8)]

    wait_lat(q0, 0)
    for p in range(PARTS):
        wait_lon(q0, 0, p)

    def first_step(r):
        for start, size in whole:
            part[r, pl.ds(start, size)] = stencil(q0, r, start, size)

    sweep(depth, 2, first_step)

    for h in range(2):
        a = recv.at[pl.ds(h * PARTNERS + 1, PARTNERS - 1), pl.ds(0, used[h])]
        pltpu.make_async_copy(a, a, recv_sem.at[h]).wait()
    place_row = lax.broadcasted_iota(jnp.int32, (rows, 128), 0)
    grid_row = (place_row % BANDS * depth + place_row // BANDS).astype(jnp.float32)
    flat = recv.reshape(recv.shape[0] * PIECE, columns)

    def taken(h, n):
        return flat[pl.ds(h * PARTNERS * PIECE + n, PARTNERS, stride=PIECE), :]

    rows_of = jnp.transpose(jnp.concatenate([taken(1, SLOTS * fields)] * SLOTS, axis=0))
    selector = []
    for h in range(2):
        own = SLOTS * (1 - h)
        named_rows = jnp.where(slot_lane < PARTNERS, rows_of[own : own + 1], rows_of[own + 1 : own + 2])
        selector.append(jnp.where(grid_row == named_rows, 1.0, 0.0).astype(jnp.bfloat16))
    selector = jnp.concatenate(selector, axis=1)

    def assemble(n):
        data = jnp.concatenate([taken(h, s * fields + n) for h in range(2) for s in range(SLOTS)], axis=0)
        high = data.astype(jnp.bfloat16)
        rest = (data - high.astype(jnp.float32)).astype(jnp.bfloat16)
        both = jnp.dot(selector, jnp.concatenate([high, rest], axis=1), preferred_element_type=jnp.float32)
        raw_force[n] = (both[:, :columns] + both[:, columns:]).reshape(depth, BANDS, columns)

    sweep(fields, 16, assemble)

    def add_forcing(r):
        forcing = jnp.transpose(raw_force[:, r].reshape(fields * BANDS, columns)) * wet[r]
        force[r] = forcing
        q1[r + EDGE, inner] = part[r] + forcing

    def sweep_from(start, count, unroll, step):
        sweep(count, unroll, lambda r: step(r + start))

    for p in range(PARTS):
        sweep_from(p * some_rows, some_rows, min(some_rows, 8), add_forcing)
        start_lon(q1, 1, p)
    start_lat(q1, 1)

    def advance(q, r, start, size):
        return stencil(q, r, start, size) + force[r, pl.ds(start, size)]

    def second(spans):
        def step(r):
            for start, size in spans:
                q2[r + EDGE, pl.ds(PAD + start, size)] = advance(q1, r, start, size)

        return step

    def third(spans):
        def step(r):
            for start, size in spans:
                part[r, pl.ds(start, size)] = advance(q2, r, start, size)

        return step

    def outside(step, part_number):
        sweep_from(part_number * some_rows, some_rows, min(some_rows, 8), step(ends))

    edge_rows = (0, 1, depth - 2, depth - 1)
    sweep_from(EDGE, depth - 2 * EDGE, 2, second(middle))
    wait_lat(q1, 1)
    for r in edge_rows:
        second(middle)(r)
    for p in range(PARTS):
        wait_lon(q1, 1, p)
        outside(second, p)
        start_lon(q2, 2, p)
    start_lat(q2, 2)
    sweep_from(EDGE, depth - 2 * EDGE, 2, third(middle))
    wait_lat(q2, 2)
    for r in edge_rows:
        third(middle)(r)
    for p in range(PARTS):
        wait_lon(q2, 2, p)
        outside(third, p)

    for step in range(STEPS):
        for p in range(PARTS):
            for copy in lon_copies(step, p):
                copy.wait_send()
        to_north, to_south = lat_copies(step)

        @pl.when(lat < 3)
        def _():
            to_north.wait_send()

        @pl.when(lat > 0)
        def _():
            to_south.wait_send()

    across.wait_send()
    for h in range(2):
        a = recv.at[pl.ds(h * PARTNERS + 1, PARTNERS - 1), pl.ds(0, used[h])]
        pltpu.make_async_copy(a, a, send_sem.at[h]).wait()


def turn_back(bands, out, result, out_sem):
    fields, _, depth, columns = out.shape
    flat = result.reshape((fields + 1) * BANDS * depth, columns)
    copies = []
    for group in range(depth // 8):
        for r in range(group * 8, group * 8 + 8):
            back = jnp.transpose(bands[r])
            for n in range(fields):
                flat[pl.ds(n * BANDS * depth + r, BANDS, stride=depth), :] = back[n * BANDS : (n + 1) * BANDS]
        rows = pl.ds(group * 8, 8)
        copy = pltpu.make_async_copy(
            result.at[pl.ds(0, fields), :, rows], out.at[:, :, rows], out_sem.at[group]
        )
        copy.start()
        copies.append(copy)
    for copy in copies:
        copy.wait()


def body(state, blocks, dest_tile, dest_row, kappa, lon_speed, lat_speed, sea_mask):
    tracers, levels, rows, columns = state.shape
    fields, depth = tracers * levels, rows // BANDS
    flat = (fields, rows, columns)
    f32, i32 = jnp.float32, jnp.int32
    anywhere = pl.BlockSpec(memory_space=pltpu.HBM)
    dma, vmem = pltpu.SemaphoreType.DMA, pltpu.VMEM
    tall = vmem((depth + 2 * EDGE, columns + 2 * PAD, 128), f32)
    turned = vmem((depth, columns, 128), f32)
    raw, coarse = vmem((fields + 1, rows, columns), f32), vmem((levels + 1, rows, columns), f32)
    bands = pl.pallas_call(
        kernel,
        out_shape=jax.ShapeDtypeStruct((depth, columns, 128), f32),
        in_specs=[anywhere] * 8,
        out_specs=pl.BlockSpec(memory_space=pltpu.VMEM),
        scratch_shapes=[
            vmem((1, 128), i32), vmem((1, 128), i32), vmem((128, fields, columns), f32),
            vmem((8, 128), i32), pltpu.SMEM((8, 128), i32), vmem((128, 128), f32),
            vmem((2, PARTNERS, PIECE, columns), f32), vmem((PARTNERS, PIECE, columns), f32),
            vmem((2 * PARTNERS + 1, PIECE, columns), f32),
            raw, coarse, coarse, coarse, vmem((levels, rows, columns), i32),
            vmem((fields, depth, BANDS, columns), f32), coarse,
            tall, tall, tall, turned, turned, turned, turned, turned,
            vmem((STEPS, 2, PARTS, EDGE * depth // PARTS, 128), f32), vmem((STEPS, 2, PARTS, EDGE * depth // PARTS, 128), f32),
            vmem((STEPS, 2, 16 * EDGE, 128), f32), vmem((STEPS, 2, 16 * EDGE, 128), f32),
            dma((8,)), dma, pltpu.SemaphoreType.REGULAR((2,)), dma, dma, dma((2,)), dma((2,)), dma((STEPS, 2 * PARTS + 2)), dma((STEPS, 2 * PARTS + 2)),
        ],
        compiler_params=pltpu.CompilerParams(
            collective_id=0, has_side_effects=True, vmem_limit_bytes=VL << 20
        ),
    )(*[
        pltpu.with_memory_space_constraint(x, pltpu.HBM)
        for x in (
            state.reshape(flat), blocks.reshape(128, fields, columns), dest_tile.reshape(1, 128),
            dest_row.reshape(1, 128), kappa, lon_speed, lat_speed, sea_mask,
        )
    ])
    result = pl.pallas_call(
        turn_back,
        out_shape=jax.ShapeDtypeStruct((fields, BANDS, depth, columns), f32),
        in_specs=[pl.BlockSpec(memory_space=pltpu.VMEM)],
        out_specs=anywhere,
        scratch_shapes=[vmem((fields + 1, BANDS, depth, columns), f32), dma((depth // 8,))],
        compiler_params=pltpu.CompilerParams(vmem_limit_bytes=16 << 20),
    )(bands)
    return result.reshape(state.shape)


def solution(mesh):
    placed = (
        P(None, None, "lat", "lon"),
        P(("lon", "lat"), None, None, None),
        P(("lon", "lat"), None),
        P(("lon", "lat")),
        P(None, "lat", "lon"),
        P(None, "lat", "lon"),
        P(None, "lat", "lon"),
        P(None, "lat", "lon"),
    )
    return jax.shard_map(
        body, mesh=mesh, in_specs=placed, out_specs=P(None, None, "lat", "lon"), check_vma=False
    )
```

```python
import jax
import jax.numpy as jnp
from jax import lax
from jax.experimental import pallas as pl
from jax.experimental.pallas import tpu as pltpu
from jax.sharding import PartitionSpec as P

MESH = pl.DeviceIdType.MESH
STEPS = 3
BANDS = 8
PARTNERS = 64
SLOTS = 2
PIECE = 40
VL = 44
PAD = 8
EDGE = 2
PARTS = 4
OFFSETS = sorted(
    ((z, x, y) for z in range(4) for x in range(4) for y in range(4)),
    key=lambda o: (sum(d > 0 for d in o), -sum(d == 2 for d in o), (16 * o[0] + 4 * o[1] + o[2]) * 27 % 64),
)
LINES, PLANES = 10, 37
Z_LINE = [i for i in range(1, LINES) if OFFSETS[i][0] > 0]
X_LINE = [i for i in range(1, LINES) if OFFSETS[i][1] > 0]


def roll(x, amount):
    amount = amount % 128
    return x if amount == 0 else pltpu.roll(x, amount, 1)


def kernel(
    state, blocks, tile_at, row_at, kappa, lon_speed, lat_speed, mask, part,
    tile_ref, row_ref, held, table, table_s, plan, send, relay, recv,
    raw_state, raw_diff, raw_zonal, raw_merid, raw_wet, raw_force, scaled,
    q0, q1, q2, force, diff, zonal, merid, wet, lon_out, lon_in, lat_out, lat_in,
    load_sem, table_sem, line_sem, core_send, core_recv, send_sem, recv_sem, halo_send, halo_recv,
):
    levels, rows, columns = kappa.shape
    fields = state.shape[0]
    depth = rows // BANDS
    used = (SLOTS * fields, SLOTS * fields + 1)
    lon, lat = lax.axis_index("lon"), lax.axis_index("lat")
    core = lat % 2
    z, x, y = lon // 8, (lat // 2) * 2 + (lon // 4) % 2, lon % 4
    other = (lon, lat + 1 - 2 * core)

    def place(i):
        dz, dx, dy = OFFSETS[i]
        return (z + dz) % 4, (x + dx) % 4, (y + dy) % 4

    def partner(i):
        z, x, y = place(i)
        return (z * 8 + (x % 2) * 4 + y, (x // 2) * 2 + core)

    moves = (
        (tile_at, tile_ref), (row_at, row_ref), (blocks, held), (state, raw_state.at[pl.ds(0, fields)]),
        (kappa, raw_diff.at[pl.ds(0, levels)]), (lon_speed, raw_zonal.at[pl.ds(0, levels)]),
        (lat_speed, raw_merid.at[pl.ds(0, levels)]), (mask, raw_wet),
    )
    loads = [pltpu.make_async_copy(src, dst, load_sem.at[k]) for k, (src, dst) in enumerate(moves)]
    east, west = ((lon + 1) % 32, lat), ((lon + 31) % 32, lat)

    barrier = pltpu.get_barrier_semaphore()
    for device in [partner(i) for i in range(1, LINES)] + [other, (lon, 3 - lat), east, west]:
        pl.semaphore_signal(barrier, inc=1, device_id=device, device_id_type=MESH)
    for copy in loads[:4]:
        copy.start()
    loads[0].wait()
    loads[1].wait()

    tile_of = lax.broadcasted_iota(jnp.int32, (128, 128), 0)
    number = lax.broadcasted_iota(jnp.int32, (128, 128), 1)
    named = tile_ref[...] == tile_of
    first = jnp.min(jnp.where(named, number, 128), axis=1, keepdims=True)
    last = jnp.max(jnp.where(named, number, -1), axis=1, keepdims=True)
    row_f = row_ref[...].astype(jnp.float32)
    first_row = jnp.sum(jnp.where(number == first, row_f, 0.0), axis=1, keepdims=True)
    last_row = jnp.sum(jnp.where(number == last, row_f, 0.0), axis=1, keepdims=True)
    first_row = jnp.where(last >= 0, first_row, -1.0)
    last_row = jnp.where(last > first, last_row, -1.0)
    plan[...] = jnp.where(number % SLOTS == 0, first_row, last_row)
    slots = jnp.where(number == 0, jnp.minimum(first, 127), jnp.maximum(last, 0))
    table[...] = jnp.transpose(slots)[:8]
    to_scalars = pltpu.make_async_copy(table, table_s, table_sem)
    to_scalars.start()
    loads[2].wait()
    to_scalars.wait()

    def tile(h, i):
        tz, tx, ty = place(i)
        return tz * 32 + (tx % 2) * 16 + ty * 4 + (tx // 2) * 2 + (core if h == 0 else 1 - core)

    def pack(h, numbers):
        for i in numbers:
            for s in range(SLOTS):
                send[h, i, pl.ds(s * fields, fields)] = held[table_s[s, tile(h, i)]]
            if h == 1:
                send[h, i, pl.ds(SLOTS * fields, 1)] = plan[pl.ds(tile(h, i), 1), :]

    pack(1, range(PARTNERS))
    pack(0, range(PARTNERS))

    def turned(ref, r):
        flat = ref.reshape(ref.shape[0] * rows, columns)
        count = ref.shape[0] - 1
        taken = [flat[pl.ds(n * rows + r, BANDS, stride=depth), :] for n in range(count)]
        return jnp.transpose(jnp.concatenate(taken * (fields // count), axis=0))

    def sweep(count, unroll, step):
        def some(i, carry):
            for k in range(unroll):
                step(i * unroll + k)
            return carry

        lax.fori_loop(0, count // unroll, some, 0)

    inner = pl.ds(PAD, columns)

    lanes = lax.broadcasted_iota(jnp.int32, (8, 128), 1)

    def halo_copy(src, dst, step, k, device):
        return pltpu.make_async_remote_copy(
            src_ref=src, dst_ref=dst, send_sem=halo_send.at[step, k], recv_sem=halo_recv.at[step, k],
            device_id=device, device_id_type=MESH,
        )

    def lon_copies(step, p):
        return [
            halo_copy(lon_out.at[step, d, p], lon_in.at[step, d, p], step, 2 * p + d, device)
            for d, device in enumerate((east, west))
        ]

    def lat_copies(step):
        return [
            halo_copy(lat_out.at[step, d], lat_in.at[step, d], step, 2 * PARTS + d, (lon, there))
            for d, there in enumerate((jnp.minimum(lat + 1, 3), jnp.maximum(lat - 1, 0)))
        ]

    some_rows = depth // PARTS

    def start_lon(q, step, p):
        for k in range(some_rows):
            n, at = EDGE + p * some_rows + k, pl.ds(EDGE * k, EDGE)
            lon_out[step, 0, p, at] = q[n, pl.ds(PAD + columns - EDGE, EDGE)]
            lon_out[step, 1, p, at] = q[n, pl.ds(PAD, EDGE)]
        for copy in lon_copies(step, p):
            copy.start()

    def start_lat(q, step):
        for k in range(EDGE):
            for half in range(2):
                up, down = jnp.zeros((8, 128), jnp.float32), jnp.zeros((8, 128), jnp.float32)
                for g in range(BANDS):
                    at = pl.ds(PAD + 8 * (half * BANDS + g), 8)
                    top, bottom = q[depth + k, at], q[EDGE + k, at]
                    q[k, at] = roll(top, 1)
                    q[EDGE + depth + k, at] = roll(bottom, -1)
                    up = jnp.where(lanes % BANDS == g, roll(top, g + 1 - BANDS), up)
                    down = jnp.where(lanes % BANDS == g, roll(bottom, g), down)
                lat_out[step, 0, pl.ds(8 * (2 * k + half), 8)] = up
                lat_out[step, 1, pl.ds(8 * (2 * k + half), 8)] = down
        to_north, to_south = lat_copies(step)

        @pl.when(lat < 3)
        def _():
            to_north.start()

        @pl.when(lat > 0)
        def _():
            to_south.start()

    def wait_lon(q, step, p):
        for copy in lon_copies(step, p):
            copy.wait_recv()
        for k in range(some_rows):
            n, at = EDGE + p * some_rows + k, pl.ds(EDGE * k, EDGE)
            q[n, pl.ds(PAD - EDGE, EDGE)] = lon_in[step, 0, p, at]
            q[n, pl.ds(PAD + columns, EDGE)] = lon_in[step, 1, p, at]

    def wait_lat(q, step):
        to_north, to_south = lat_copies(step)

        @pl.when(lat < 3)
        def _():
            to_south.wait_recv()

        @pl.when(lat > 0)
        def _():
            to_north.wait_recv()

        for k in range(EDGE):
            for half in range(2):
                below = lat_in[step, 0, pl.ds(8 * (2 * k + half), 8)]
                above = lat_in[step, 1, pl.ds(8 * (2 * k + half), 8)]
                for g in range(BANDS):
                    at = pl.ds(PAD + 8 * (half * BANDS + g), 8)
                    q[k, at] = jnp.where(lanes % BANDS == 0, roll(below, -g), q[k, at])
                    n = EDGE + depth + k
                    q[n, at] = jnp.where(lanes % BANDS == BANDS - 1, roll(above, BANDS - 1 - g), q[n, at])

    blank = jnp.zeros(lat_in.shape[2:], jnp.float32)
    for step in range(STEPS):

        @pl.when(lat == 0)
        def _():
            lat_in[step, 0] = blank

        @pl.when(lat == 3)
        def _():
            lat_in[step, 1] = blank


    across = pltpu.make_async_remote_copy(
        src_ref=send.at[1, :, pl.ds(0, used[1])], dst_ref=relay.at[:, pl.ds(0, used[1])],
        send_sem=core_send, recv_sem=core_recv, device_id=other, device_id_type=MESH,
    )

    slot_lane = lax.broadcasted_iota(jnp.int32, (1, 128), 1)

    def post(h, numbers):
        for i in numbers:
            src = send.at[0, i] if h == 0 else relay.at[i]
            pltpu.make_async_remote_copy(
                src_ref=src.at[pl.ds(0, used[h])], dst_ref=recv.at[h * PARTNERS + i, pl.ds(0, used[h])],
                send_sem=send_sem.at[h], recv_sem=recv_sem.at[h], device_id=partner(i), device_id_type=MESH,
            ).start()

    pl.semaphore_wait(barrier, LINES + 3)
    for i in Z_LINE + X_LINE:
        pl.semaphore_signal(line_sem.at[0], inc=1, device_id=partner(i), device_id_type=MESH)
    across.start()
    post(0, range(1, LINES))
    for copy in loads[4:]:
        copy.start()
    recv[0] = send[0, 0]

    loads[3].wait()

    def turn_state(r):
        q0[r + EDGE, inner] = turned(raw_state, r)

    sweep(depth, 8, turn_state)

    for p in range(PARTS):
        start_lon(q0, 0, p)
    start_lat(q0, 0)
    pl.semaphore_wait(line_sem.at[0], len(Z_LINE + X_LINE))
    for i in Z_LINE:
        pl.semaphore_signal(line_sem.at[1], inc=1, device_id=partner(i), device_id_type=MESH)
    post(0, range(LINES, PLANES))
    pl.semaphore_wait(line_sem.at[1], len(Z_LINE))
    post(0, range(PLANES, PARTNERS))
    across.wait_recv()
    for i in range(PARTNERS):
        at = (i, pl.ds(SLOTS * fields, 1))
        relay[at] = jnp.where(slot_lane < SLOTS, relay[at], plan[pl.ds(tile(0, i), 1), :])
    recv[PARTNERS] = relay[0]
    for numbers in (range(PLANES, PARTNERS), range(LINES, PLANES), range(1, LINES)):
        post(1, numbers)


    for copy in loads[4:]:
        copy.wait()

    def scale(n, carry):
        for b in range(rows // 32):
            at = (n, pl.ds(b * 32, 32))
            sea = raw_wet[at].astype(jnp.float32)
            raw_diff[at] = raw_diff[at] * sea
            raw_zonal[at] = raw_zonal[at] * sea * (1.0 / 12.0)
            raw_merid[at] = raw_merid[at] * sea * (1.0 / 12.0)
            scaled[at] = sea * (1.0 / STEPS)
        return carry

    lax.fori_loop(0, levels, scale, 0)
    for raw, ref in ((raw_diff, diff), (raw_zonal, zonal), (raw_merid, merid), (scaled, wet)):

        def turn(r):
            ref[r] = turned(raw, r)

        sweep(depth, 8, turn)

    def stencil(q, r, start, size):
        n, here_at = r + EDGE, pl.ds(PAD + start, size)
        here = q[n, here_at]
        east_cell, west_cell = q[n, pl.ds(PAD + start + 1, size)], q[n, pl.ds(PAD + start - 1, size)]
        far_east, far_west = q[n, pl.ds(PAD + start + 2, size)], q[n, pl.ds(PAD + start - 2, size)]
        north_cell, south_cell = q[n + 1, here_at], q[n - 1, here_at]
        far_north, far_south = q[n + 2, here_at], q[n - 2, here_at]
        at = (r, pl.ds(start, size))
        laplace = (east_cell + west_cell) + (north_cell + south_cell) - 4.0 * here
        along = 8.0 * (east_cell - west_cell) - (far_east - far_west)
        across = 8.0 * (north_cell - south_cell) - (far_north - far_south)
        return here + diff[at] * laplace - zonal[at] * along - merid[at] * across

    whole = [(32 * b, 32) for b in range(columns // 32)]
    middle = [(8, 32), (40, 32), (72, 32), (104, 16)]
    ends = [(0, 8), (columns - 8, 8)]

    wait_lat(q0, 0)
    for p in range(PARTS):
        wait_lon(q0, 0, p)

    def first_step(r):
        for start, size in whole:
            part[r, pl.ds(start, size)] = stencil(q0, r, start, size)

    sweep(depth, 2, first_step)

    for h in range(2):
        a = recv.at[pl.ds(h * PARTNERS + 1, PARTNERS - 1), pl.ds(0, used[h])]
        pltpu.make_async_copy(a, a, recv_sem.at[h]).wait()
    place_row = lax.broadcasted_iota(jnp.int32, (rows, 128), 0)
    grid_row = (place_row % BANDS * depth + place_row // BANDS).astype(jnp.float32)
    flat = recv.reshape(recv.shape[0] * PIECE, columns)

    def taken(h, n):
        return flat[pl.ds(h * PARTNERS * PIECE + n, PARTNERS, stride=PIECE), :]

    rows_of = jnp.transpose(jnp.concatenate([taken(1, SLOTS * fields)] * SLOTS, axis=0))
    selector = []
    for h in range(2):
        own = SLOTS * (1 - h)
        named_rows = jnp.where(slot_lane < PARTNERS, rows_of[own : own + 1], rows_of[own + 1 : own + 2])
        selector.append(jnp.where(grid_row == named_rows, 1.0, 0.0).astype(jnp.bfloat16))
    selector = jnp.concatenate(selector, axis=1)

    def assemble(n):
        data = jnp.concatenate([taken(h, s * fields + n) for h in range(2) for s in range(SLOTS)], axis=0)
        high = data.astype(jnp.bfloat16)
        rest = (data - high.astype(jnp.float32)).astype(jnp.bfloat16)
        both = jnp.dot(selector, jnp.concatenate([high, rest], axis=1), preferred_element_type=jnp.float32)
        raw_force[n] = (both[:, :columns] + both[:, columns:]).reshape(depth, BANDS, columns)

    sweep(fields, 16, assemble)

    def add_forcing(r):
        forcing = jnp.transpose(raw_force[:, r].reshape(fields * BANDS, columns)) * wet[r]
        force[r] = forcing
        q1[r + EDGE, inner] = part[r] + forcing

    def sweep_from(start, count, unroll, step):
        sweep(count, unroll, lambda r: step(r + start))

    for p in range(PARTS):
        sweep_from(p * some_rows, some_rows, min(some_rows, 8), add_forcing)
        start_lon(q1, 1, p)
    start_lat(q1, 1)

    def advance(q, r, start, size):
        return stencil(q, r, start, size) + force[r, pl.ds(start, size)]

    def second(spans):
        def step(r):
            for start, size in spans:
                q2[r + EDGE, pl.ds(PAD + start, size)] = advance(q1, r, start, size)

        return step

    def third(spans):
        def step(r):
            for start, size in spans:
                part[r, pl.ds(start, size)] = advance(q2, r, start, size)

        return step

    def outside(step, part_number):
        sweep_from(part_number * some_rows, some_rows, min(some_rows, 8), step(ends))

    edge_rows = (0, 1, depth - 2, depth - 1)
    sweep_from(EDGE, depth - 2 * EDGE, 4, second(middle))
    wait_lat(q1, 1)
    for r in edge_rows:
        second(middle)(r)
    for p in range(PARTS):
        wait_lon(q1, 1, p)
        outside(second, p)
        start_lon(q2, 2, p)
    start_lat(q2, 2)
    sweep_from(EDGE, depth - 2 * EDGE, 4, third(middle))
    wait_lat(q2, 2)
    for r in edge_rows:
        third(middle)(r)
    for p in range(PARTS):
        wait_lon(q2, 2, p)
        outside(third, p)

    for step in range(STEPS):
        for p in range(PARTS):
            for copy in lon_copies(step, p):
                copy.wait_send()
        to_north, to_south = lat_copies(step)

        @pl.when(lat < 3)
        def _():
            to_north.wait_send()

        @pl.when(lat > 0)
        def _():
            to_south.wait_send()

    across.wait_send()
    for h in range(2):
        a = recv.at[pl.ds(h * PARTNERS + 1, PARTNERS - 1), pl.ds(0, used[h])]
        pltpu.make_async_copy(a, a, send_sem.at[h]).wait()


def turn_back(bands, out, result, out_sem):
    fields, _, depth, columns = out.shape
    flat = result.reshape((fields + 1) * BANDS * depth, columns)
    copies = []
    for group in range(depth // 8):
        for r in range(group * 8, group * 8 + 8):
            back = jnp.transpose(bands[r])
            for n in range(fields):
                flat[pl.ds(n * BANDS * depth + r, BANDS, stride=depth), :] = back[n * BANDS : (n + 1) * BANDS]
        rows = pl.ds(group * 8, 8)
        copy = pltpu.make_async_copy(
            result.at[pl.ds(0, fields), :, rows], out.at[:, :, rows], out_sem.at[group]
        )
        copy.start()
        copies.append(copy)
    for copy in copies:
        copy.wait()


def body(state, blocks, dest_tile, dest_row, kappa, lon_speed, lat_speed, sea_mask):
    tracers, levels, rows, columns = state.shape
    fields, depth = tracers * levels, rows // BANDS
    flat = (fields, rows, columns)
    f32, i32 = jnp.float32, jnp.int32
    anywhere = pl.BlockSpec(memory_space=pltpu.HBM)
    dma, vmem = pltpu.SemaphoreType.DMA, pltpu.VMEM
    tall = vmem((depth + 2 * EDGE, columns + 2 * PAD, 128), f32)
    turned = vmem((depth, columns, 128), f32)
    raw, coarse = vmem((fields + 1, rows, columns), f32), vmem((levels + 1, rows, columns), f32)
    bands = pl.pallas_call(
        kernel,
        out_shape=jax.ShapeDtypeStruct((depth, columns, 128), f32),
        in_specs=[anywhere] * 8,
        out_specs=pl.BlockSpec(memory_space=pltpu.VMEM),
        scratch_shapes=[
            vmem((1, 128), i32), vmem((1, 128), i32), vmem((128, fields, columns), f32),
            vmem((8, 128), i32), pltpu.SMEM((8, 128), i32), vmem((128, 128), f32),
            vmem((2, PARTNERS, PIECE, columns), f32), vmem((PARTNERS, PIECE, columns), f32),
            vmem((2 * PARTNERS + 1, PIECE, columns), f32),
            raw, coarse, coarse, coarse, vmem((levels, rows, columns), i32),
            vmem((fields, depth, BANDS, columns), f32), coarse,
            tall, tall, tall, turned, turned, turned, turned, turned,
            vmem((STEPS, 2, PARTS, EDGE * depth // PARTS, 128), f32), vmem((STEPS, 2, PARTS, EDGE * depth // PARTS, 128), f32),
            vmem((STEPS, 2, 16 * EDGE, 128), f32), vmem((STEPS, 2, 16 * EDGE, 128), f32),
            dma((8,)), dma, pltpu.SemaphoreType.REGULAR((2,)), dma, dma, dma((2,)), dma((2,)), dma((STEPS, 2 * PARTS + 2)), dma((STEPS, 2 * PARTS + 2)),
        ],
        compiler_params=pltpu.CompilerParams(
            collective_id=0, has_side_effects=True, vmem_limit_bytes=VL << 20
        ),
    )(*[
        pltpu.with_memory_space_constraint(x, pltpu.HBM)
        for x in (
            state.reshape(flat), blocks.reshape(128, fields, columns), dest_tile.reshape(1, 128),
            dest_row.reshape(1, 128), kappa, lon_speed, lat_speed, sea_mask,
        )
    ])
    result = pl.pallas_call(
        turn_back,
        out_shape=jax.ShapeDtypeStruct((fields, BANDS, depth, columns), f32),
        in_specs=[pl.BlockSpec(memory_space=pltpu.VMEM)],
        out_specs=anywhere,
        scratch_shapes=[vmem((fields + 1, BANDS, depth, columns), f32), dma((depth // 8,))],
        compiler_params=pltpu.CompilerParams(vmem_limit_bytes=16 << 20),
    )(bands)
    return result.reshape(state.shape)


def solution(mesh):
    placed = (
        P(None, None, "lat", "lon"),
        P(("lon", "lat"), None, None, None),
        P(("lon", "lat"), None),
        P(("lon", "lat")),
        P(None, "lat", "lon"),
        P(None, "lat", "lon"),
        P(None, "lat", "lon"),
        P(None, "lat", "lon"),
    )
    return jax.shard_map(
        body, mesh=mesh, in_specs=placed, out_specs=P(None, None, "lat", "lon"), check_vma=False
    )
```
